32 devices in a mesh: dp: 2 (over y), row: 4 (over z), col: 4 (over x, core).
Axes of the slice: x: 2, y: 2, z: 4, core: 2. Of those that a mesh axis runs over, the one named last changes fastest.
Arguments:
- first_view: bfloat16 [2048, 8192], P('dp', ('row', 'col')), may hold values from -6 to 6
- second_view: bfloat16 [2048, 8192], P('dp', ('row', 'col')), may hold values from -6 to 6
Outputs:
- loss: float32 [], replicated
- grad_first: float32 [2048, 8192], P('dp', ('row', 'col'))
- grad_second: float32 [2048, 8192], P('dp', ('row', 'col'))
The draws below stay inside these ranges and needn't reach their ends.
All inputs are finite; a program needn't handle non-finite values.
Results may differ from the reference program's by a relative error of at most 0.00085.
Values may be sent and summed in bfloat16 or wider, within the bound.
No kernel may reach another device: no remote copies, remote signals or barrier semaphores. Data moves between devices by JAX's collectives and lax.ppermute only.
A program may use at most 192 MiB of HBM per device.

```python
import jax
import jax.numpy as jnp
from jax import lax

F = 8192
TOKENS = 2048


def steps_of(rng, extent, cuts, least, top_value):
    loudness, own = 1.0, jax.random.fold_in(rng, 6)
    for axis_at, parts in cuts:
        heights = jnp.exp(jax.random.uniform(jax.random.fold_in(own, axis_at), (parts,), jnp.float32, least / len(cuts), top_value / len(cuts)))
        loudness = loudness * jnp.repeat(heights, extent[axis_at] // parts).reshape([-1 if axis == axis_at else 1 for axis in range(len(extent))])
    return loudness


def gaussian(stream_key, shape, deviation, reach, split=(), kind=jnp.bfloat16):
    level = steps_of(stream_key, shape, split, -0.22, 0.18) if split else 1.0
    result = jax.random.normal(stream_key, shape, jnp.float32) * deviation * level
    return jnp.minimum(jnp.maximum(result, -reach), reach).astype(kind)


def setup_inputs(seed: int = 0) -> dict:
    splits = jax.random.split(jax.random.key(seed), 3)
    return {
        "first_view": gaussian(splits[0], (TOKENS, F), 1.0, 6.0, ((0, 2), (1, 16))),
        "second_view": gaussian(splits[1], (TOKENS, F), 1.0, 6.0, ((0, 2), (1, 16))),
    }


inv_weight = 25.0
var_weight = 25.0
cov_weight = 1.0
eps_var = 0.0001

def prepare(embed):
    mean_row = lax.optimization_barrier(jnp.sum(embed, axis=0)) / TOKENS
    centred = embed - mean_row
    variance = lax.optimization_barrier(jnp.sum(centred * centred, axis=0)) / (TOKENS - 1)
    spread = jnp.sqrt(variance + eps_var)
    hinge = jnp.maximum(1.0 - spread, 0.0)
    rounded = centred.astype(jnp.bfloat16)
    return (centred, spread, hinge, rounded)

def covariance_terms(rounded):
    block = min(F, 1024)
    count = F // block

    def one_block(index):
        start = (index * block).astype(jnp.int32)
        rows = lax.dynamic_slice_in_dim(rounded, start, block, 1)
        tile = lax.dot_general(rows, rounded, (((0,), (0,)), ((), ())), preferred_element_type=jnp.float32) / (TOKENS - 1)
        diag = jnp.arange(F, dtype=jnp.int32)[None, :] == (start + jnp.arange(block, dtype=jnp.int32))[:, None]
        offdiag = jnp.where(diag, jnp.float32(0.0), tile)
        square = jnp.sum(offdiag * offdiag)
        product = lax.dot_general(rounded, offdiag.astype(jnp.bfloat16), (((1,), (1,)), ((), ())), preferred_element_type=jnp.float32)
        return (square, product)
    squares, products = lax.map(one_block, jnp.arange(count, dtype=jnp.int32))
    product_all = jnp.transpose(products, (1, 0, 2)).reshape(TOKENS, F)
    return (jnp.sum(squares), product_all)

def reference(first_view, second_view):
    first = first_view.astype(jnp.float32)
    second = second_view.astype(jnp.float32)
    cen_first, spr_first, hin_first, rnd_first = prepare(first)
    cen_second, spr_second, hin_second, rnd_second = prepare(second)
    sq_first, prod_first = covariance_terms(rnd_first)
    sq_second, prod_second = covariance_terms(rnd_second)
    differ = first - second
    loss = inv_weight * jnp.sum(differ * differ) / (TOKENS * F) + var_weight * (jnp.sum(hin_first) + jnp.sum(hin_second)) / F + cov_weight * (sq_first + sq_second) / F
    scale = TOKENS * F / 64.0

    def gradient(sign, centred, spread, product):
        invariant = sign * 2.0 * inv_weight * differ / (TOKENS * F)
        active = jnp.where(spread < 1.0, jnp.float32(1.0), jnp.float32(0.0))
        varterm = -var_weight * centred * active / (F * spread * (TOKENS - 1))
        covterm = 4.0 * cov_weight * product / (F * (TOKENS - 1))
        return scale * (invariant + varterm + covterm)
    return (loss, gradient(1.0, cen_first, spr_first, prod_first), gradient(-1.0, cen_second, spr_second, prod_second))
```

```python
import jax
import jax.numpy as jnp
from jax import lax
from jax.sharding import PartitionSpec as P

inv_weight = 25.0
var_weight = 25.0
cov_weight = 1.0
eps_var = 0.0001


def shift(value, axis, count, step, inner):
    pairs = [
        (index, (index // inner + step) % count * inner + index % inner)
        for index in range(count * inner)
    ]
    return lax.ppermute(value, axis, pairs)


def core_swap(value):
    return lax.ppermute(value, "col", [(index, index ^ 1) for index in range(lax.axis_size("col"))])


def part(value, index, count):
    size = value.shape[0] // count
    return lax.dynamic_slice_in_dim(value, index * size, size, 0)


def scatter_sum(value, axis, count, inner, place):
    total = part(value, place, count).astype(jnp.float32)
    for step in range(1, count):
        sent = part(value, (place + step) % count, count).astype(jnp.bfloat16)
        total = total + shift(sent, axis, count, step, inner).astype(jnp.float32)
    return total


def collect(value, axis, count, inner, place):
    size = value.shape[0]
    whole = jnp.zeros((count * size,) + value.shape[1:], value.dtype)
    whole = lax.dynamic_update_slice_in_dim(whole, value, place * size, 0)
    for step in range(1, count):
        got = shift(value, axis, count, step, inner)
        whole = lax.dynamic_update_slice_in_dim(whole, got, (place - step) % count * size, 0)
    return whole


def outer(left, right):
    return lax.dot_general(
        left, right, (((1,), (1,)), ((), ())), preferred_element_type=jnp.float32
    )


def matmul(left, right, dim):
    return lax.dot_general(
        left, right, (((dim,), (0,)), ((), ())), preferred_element_type=jnp.float32
    )


def on_device(first_view, second_view):
    dp_count = lax.axis_size("dp")
    row_count = lax.axis_size("row")
    col_count = lax.axis_size("col")
    rows, width = first_view.shape
    total = rows * dp_count
    feat = width * row_count * col_count
    half, quarter = rows // 2, rows // 4
    x_count = col_count // 2
    x_place = lax.axis_index("col") // 2
    core = lax.axis_index("col") % 2
    z_place = lax.axis_index("row")

    views = (first_view, second_view)
    values = [view.astype(jnp.float32) for view in views]
    sums = jnp.stack([jnp.sum(value, axis=0) for value in values])
    sums = sums + shift(sums, "dp", dp_count, 1, 1)
    others = [shift(view, "dp", dp_count, 1, 1) for view in views]
    means = [sums[index] / total for index in range(2)]
    centred = [value - mean for value, mean in zip(values, means)]
    rounded = [cen.astype(jnp.bfloat16) for cen in centred]
    partner = [core_swap(rnd) for rnd in rounded]

    def reduce_piece(piece):
        piece = scatter_sum(piece, "col", x_count, 2, x_place)
        return scatter_sum(piece, "row", row_count, 1, z_place)

    def gather_piece(chunk):
        piece = collect(chunk, "row", row_count, 1, z_place)
        piece = collect(piece, "col", x_count, 2, x_place)
        return piece, core_swap(piece)

    def weighted_squares(chunk, doubled_from, piece_rows):
        size = chunk.shape[0]
        ids = (x_place * row_count + z_place) * size + jnp.arange(size, dtype=jnp.int32)
        weight = jnp.where(ids < doubled_from, jnp.float32(1.0), jnp.float32(2.0))
        return jnp.sum(chunk * chunk * weight[:, None])

    eye = jnp.eye(half, dtype=jnp.bool_)
    near = []
    lengths = []
    squares = jnp.float32(0.0)
    for index in range(2):
        both = jnp.concatenate([rounded[index], partner[index]], axis=1)
        wide = both.astype(jnp.float32)
        lengths.append(jnp.sum(wide * wide, axis=1))
        block = part(both, core, 2)
        diagonal = jnp.where(eye, jnp.float32(0.0), outer(block, block))
        cross = outer(part(both[:half], core, 2), both[half:])
        chunk = reduce_piece(jnp.concatenate([diagonal, cross], axis=0))
        squares = squares + weighted_squares(chunk, half, half + quarter)
        near.append(gather_piece(chunk.astype(jnp.bfloat16)))
    lengths = jnp.stack(lengths)
    for axis, count, inner in (("col", x_count, 2), ("row", row_count, 1)):
        lengths = lengths + sum(shift(lengths, axis, count, step, inner) for step in range(1, count))

    far = []
    cen_others, rnd_others = [], []
    for index in range(2):
        cen_other = others[index].astype(jnp.float32) - means[index]
        rnd_other = cen_other.astype(jnp.bfloat16)
        cen_others.append(cen_other)
        rnd_others.append(rnd_other)
        both = jnp.concatenate([rounded[index], partner[index]], axis=1)
        both_other = jnp.concatenate([rnd_other, core_swap(rnd_other)], axis=1)
        block = part(both, core, 2)
        piece = jnp.concatenate(
            [outer(block, both_other[:half]), outer(block, both_other[half:])], axis=0
        )
        chunk = reduce_piece(piece)
        squares = squares + jnp.sum(chunk * chunk)
        far.append(gather_piece(chunk.astype(jnp.bfloat16)))

    differ = values[0] - values[1]
    scale = total * feat / 64.0
    hinge_sum = jnp.float32(0.0)
    norm_sum = jnp.float32(0.0)
    grads = []
    for index in range(2):
        sq_own = jnp.sum(centred[index] * centred[index], axis=0)
        sq_other = jnp.sum(cen_others[index] * cen_others[index], axis=0)
        spread = jnp.sqrt((sq_own + sq_other) / (total - 1) + eps_var)
        hinge_sum = hinge_sum + jnp.sum(jnp.maximum(1.0 - spread, 0.0))
        rnd, rnd_other = rounded[index], rnd_others[index]
        norms = jnp.sum(jnp.square(rnd.astype(jnp.float32)), axis=0) + jnp.sum(
            jnp.square(rnd_other.astype(jnp.float32)), axis=0
        )
        norm_sum = norm_sum + jnp.sum(jnp.square(norms / (total - 1)))
        mine, theirs = near[index]
        low = jnp.where(core == 0, mine, theirs)
        high = jnp.where(core == 0, theirs, mine)
        cross = jnp.concatenate([low[half:], high[half:]], axis=0)
        far_low = jnp.where(core == 0, far[index][0], far[index][1])
        far_high = jnp.where(core == 0, far[index][1], far[index][0])
        top = (
            matmul(low[:half], rnd[:half], 1)
            + matmul(cross, rnd[half:], 1)
            + matmul(far_low[:half], rnd_other[:half], 1)
            + matmul(far_low[half:], rnd_other[half:], 1)
        )
        bottom = (
            matmul(high[:half], rnd[half:], 1)
            + matmul(cross, rnd[:half], 0)
            + matmul(far_high[:half], rnd_other[:half], 1)
            + matmul(far_high[half:], rnd_other[half:], 1)
        )
        product = jnp.concatenate([top, bottom], axis=0)
        product = (
            product + (lengths[index][:, None] - norms[None, :]) * rnd.astype(jnp.float32)
        ) / (total - 1)
        sign = 1.0 - 2.0 * index
        invariant = sign * 2.0 * inv_weight * differ / (total * feat)
        active = jnp.where(spread < 1.0, jnp.float32(1.0), jnp.float32(0.0))
        varterm = -var_weight * centred[index] * active / (feat * spread * (total - 1))
        covterm = 4.0 * cov_weight * product / (feat * (total - 1))
        grads.append(scale * (invariant + varterm + covterm))

    length_sum = jnp.sum(jnp.square(lengths / (total - 1)))
    cov_part = (
        squares / (total - 1) / (total - 1)
        + length_sum / (row_count * col_count)
        - norm_sum / dp_count
    ) / feat
    local_loss = (
        inv_weight * jnp.sum(differ * differ) / (total * feat)
        + var_weight * hinge_sum / feat / dp_count
        + cov_weight * cov_part
    )
    loss = lax.psum(local_loss, ("dp", "row", "col"))
    return loss, grads[0], grads[1]


def solution(mesh):
    return jax.shard_map(
        on_device,
        mesh=mesh,
        in_specs=(P("dp", ("row", "col")), P("dp", ("row", "col"))),
        out_specs=(P(), P("dp", ("row", "col")), P("dp", ("row", "col"))),
        check_vma=False,
    )
```

```python
import functools

import jax
import jax.numpy as jnp
from jax import lax
from jax.experimental import pallas as pl
from jax.experimental.pallas import tpu as pltpu
from jax.sharding import PartitionSpec as P

inv_weight = 25.0
var_weight = 25.0
cov_weight = 1.0
eps_var = 0.0001

VMEM = pl.BlockSpec(memory_space=pltpu.VMEM)
SMEM = pl.BlockSpec(memory_space=pltpu.SMEM)
PARAMS = pltpu.CompilerParams(vmem_limit_bytes=16 * 1024 * 1024)


class Chain:
    def __init__(self):
        self.last = None

    def __call__(self, kernel, outs, ins, scratch=()):
        specs = [SMEM if x.ndim == 1 else VMEM for x in ins]
        body = kernel
        if self.last is not None:
            ins, specs = [self.last] + list(ins), [pl.BlockSpec(memory_space=pl.ANY)] + specs

            def body(_, *refs):
                kernel(*refs)

        outs = pl.pallas_call(
            body,
            out_shape=outs,
            in_specs=specs,
            out_specs=[SMEM if out.shape == (1,) else VMEM for out in outs],
            scratch_shapes=scratch,
            compiler_params=PARAMS,
            cost_estimate=pl.CostEstimate(flops=1, bytes_accessed=1, transcendentals=0),
        )(*ins)
        self.last = outs[0]
        return outs


def array(shape, dtype):
    return jax.ShapeDtypeStruct(shape, dtype)


def shift(value, axis, count, step, inner):
    pairs = [
        (index, (index // inner + step) % count * inner + index % inner)
        for index in range(count * inner)
    ]
    return lax.ppermute(value, axis, pairs)


def partner_of(value, axis, bit):
    return lax.ppermute(value, axis, [(index, index ^ bit) for index in range(lax.axis_size(axis))])


def core_swap(value):
    return partner_of(value, "col", 1)


def dot_t(left, right):
    return lax.dot_general(
        left, right, (((1,), (1,)), ((), ())), preferred_element_type=jnp.float32
    )


def dot(left, right):
    return lax.dot_general(
        left, right, (((1,), (0,)), ((), ())), preferred_element_type=jnp.float32
    )


def sums_kernel(first, second, out):
    out[0:1, :] = jnp.sum(first[...].astype(jnp.float32), axis=0, keepdims=True)
    out[1:2, :] = jnp.sum(second[...].astype(jnp.float32), axis=0, keepdims=True)


def split_rows(values, count, rows):
    width = values[0].shape[1]
    ids = lax.broadcasted_iota(jnp.int32, (rows, width), 0)
    block = jnp.zeros((rows, width), jnp.float32)
    for index, rest in enumerate(values):
        for term in range(count):
            head = rest.astype(jnp.bfloat16).astype(jnp.float32)
            block = jnp.where(ids == index * count + term, head, block)
            rest = rest - head
    return block.astype(jnp.bfloat16)


def write_extra(out, main, extra):
    if out.dtype == jnp.bfloat16:
        out[main : main + 16, :] = split_rows([extra], 2, 16)
    else:
        ids = lax.broadcasted_iota(jnp.int32, (16, extra.shape[1]), 0)
        out[main : main + 16, :] = jnp.where(ids == 0, extra, 0.0)


def read_extra(ref, main):
    block = ref[main : main + 16, :].astype(jnp.float32)
    return block[0:1, :] + block[1:2, :]


def centre_kernel(total, first, second, sums, rounded_out, stats, sent):
    rows, width = first.shape
    found = []
    squares = []
    for index, view in enumerate((first, second)):
        centred = view[...].astype(jnp.float32) - sums[index : index + 1, :] / total
        rounded = centred.astype(jnp.bfloat16)
        rounded_out[index] = rounded
        wide = rounded.astype(jnp.float32)
        found.append(jnp.sum(centred * centred, axis=0, keepdims=True))
        squares.append(jnp.sum(wide * wide, axis=0, keepdims=True))
    differ = first[...].astype(jnp.float32) - second[...].astype(jnp.float32)
    found += squares + [jnp.sum(differ * differ, axis=0, keepdims=True)]
    ids = lax.broadcasted_iota(jnp.int32, (8, width), 0)
    block = jnp.zeros((8, width), jnp.float32)
    for index, value in enumerate(found):
        block = jnp.where(ids == index, value, block)
    stats[...] = block
    sent[:rows, :] = second[...]
    sent[rows:, :] = split_rows(found, 3, 16)


def near_place(tile_index, core, rows, tile):
    half, quarter = rows // 2, rows // 4
    square = tile_index < half // tile
    row = jnp.where(square, half * core + tile * tile_index, quarter * core + tile * tile_index - half)
    column = jnp.where(square, half * core, half)
    return square, pl.multiple_of(row, tile), pl.multiple_of(column, half)


def near_kernel(x_count, view, place, own, *rest):
    (top, bottom), (partner, keep, *sends) = rest[:2], rest[2:]
    core, x_place = place[0], place[1]
    rows = own.shape[1]
    half = rows // 2
    tile = rows // 4 // x_count
    partner[:half, :] = top[...]
    partner[half:, :] = bottom[...]
    row_ids = lax.broadcasted_iota(jnp.int32, (tile, half), 0)
    column_ids = lax.broadcasted_iota(jnp.int32, (tile, half), 1)
    for step in range(x_count):
        out = keep if step == 0 else sends[step - 1]
        extra = jnp.zeros((1, half), jnp.float32)
        for piece in range(3):
            index = (x_place + step) % x_count * 3 + piece
            square, row, column = near_place(index, core, rows, tile)
            diagonal = jnp.logical_and(square, column_ids == row_ids + tile * index)
            value = dot_t(own[view, pl.ds(row, tile), :], own[view, pl.ds(column, half), :])
            value = value + dot_t(
                partner[pl.ds(row, tile), :], partner[pl.ds(column, half), :]
            )
            extra = extra + jnp.sum(jnp.where(diagonal, value, 0.0), axis=0, keepdims=True)
            value = jnp.where(diagonal, 0.0, value)
            out[pl.ds(piece * tile, tile), :] = value.astype(out.dtype)
        write_extra(out, 3 * tile, extra)


def centre_other_kernel(total, index, other, sums, *outs):
    mean = sums[index : index + 1, :] / total
    stats = None
    if index == 1:
        stats, outs = outs[0], outs[1:]
    size = outs[0].shape[0]
    for step in range(4):
        at = slice(step * size, (step + 1) * size)
        outs[step][...] = (other[at, :].astype(jnp.float32) - mean).astype(jnp.bfloat16)
    if stats is not None:
        block = other[4 * size :, :].astype(jnp.float32)
        ids = lax.broadcasted_iota(jnp.int32, stats.shape, 0)
        value = jnp.zeros(stats.shape, jnp.float32)
        for row in range(5):
            at = 3 * row
            got = block[at : at + 1, :] + block[at + 1 : at + 2, :] + block[at + 2 : at + 3, :]
            value = jnp.where(ids == row, got, value)
        outs[4][...] = stats[...] + value


def add_kernel(main, *refs):
    out = refs[-1]
    value = refs[0][:main, :].astype(jnp.float32)
    for ref in refs[1:-1]:
        value = value + ref[:main, :].astype(jnp.float32)
    out[:main, :] = value.astype(out.dtype)
    if main < out.shape[0]:
        extra = read_extra(refs[0], main)
        for ref in refs[1:-1]:
            extra = extra + read_extra(ref, main)
        write_extra(out, main, extra)


def pick_kernel(place, mine, got, out):
    @pl.when(place[2] == 1)
    def _():
        out[...] = mine[...]

    @pl.when(place[2] == 0)
    def _():
        out[...] = got[...]


def loss_terms(total, feat, stats):
    spread = jnp.sqrt(stats[0:2, :] / (total - 1) + eps_var)
    norms = stats[2:4, :] / (total - 1)
    return (
        inv_weight * stats[4:5, :] / (total * feat)
        + var_weight * jnp.sum(jnp.maximum(1.0 - spread, 0.0), axis=0, keepdims=True) / feat
        - cov_weight * jnp.sum(norms * norms, axis=0, keepdims=True) / feat
    )


def far_kernel(x_count, view, total, feat, place, own, partner, *rest):
    others, swapped, outs = rest[:4], rest[4:8], rest[8:]
    stats = None
    if view == 1:
        stats, outs = outs[0], outs[1:]
    core, x_place = place[0], place[1]
    half = own.shape[1] // 2
    quarter = half // 2
    tile = half // x_count
    for block in range(2):
        for step in range(x_count):
            out = outs[block * x_count + step]
            part = (x_place + step) % x_count
            row = pl.ds(pl.multiple_of(half * core + tile * part, tile), tile)
            left, left_partner = own[view, row, :], partner[row, :]
            for side in range(2):
                at = 2 * block + side
                value = dot_t(left, others[at][...]) + dot_t(left_partner, swapped[at][...])
                out[:tile, side * quarter : (side + 1) * quarter] = value.astype(out.dtype)
            if out.shape[0] > tile:
                terms = loss_terms(total, feat, stats)
                terms = jnp.where(part == 0, terms, 0.0)
                if terms.shape[1] < half:
                    terms = jnp.concatenate(
                        [terms, jnp.zeros((1, half - terms.shape[1]), jnp.float32)], axis=1
                    )
                write_extra(out, tile, terms)


def near_product_kernel(
    x_count, index, total, feat, place, rounded, first, second, sums, stats, *rest
):
    parts, (base, squares, grid, columns) = rest[:-4], rest[-4:]
    core, x_place = place[0], place[1]
    rows, width = rounded.shape[1:]
    half = rows // 2
    tile = rows // 4 // x_count
    square_sum = jnp.float32(0.0)
    for side in range(2):
        owner = core if side == 0 else 1 - core
        extra = jnp.zeros((1, half), jnp.float32)
        for step in range(x_count):
            extra = extra + read_extra(parts[side * x_count + step], 3 * tile)
            for piece in range(3):
                at = (x_place + x_count - step) % x_count * 3 + piece
                _, row, column = near_place(at, owner, rows, tile)
                grid[pl.ds(row, tile), pl.ds(column, half)] = parts[side * x_count + step][
                    pl.ds(piece * tile, tile), :
                ]
        square_sum = square_sum + jnp.sum(extra * extra)
        columns[pl.ds(pl.multiple_of(half * owner, half), half), :] = jnp.broadcast_to(
            extra, (8, half)
        ).T
    grid[half:, :half] = grid[:half, half:].T
    scale = total * feat / 64.0
    spread = jnp.sqrt(stats[index : index + 1, :] / (total - 1) + eps_var)
    active = jnp.where(spread < 1.0, 1.0, 0.0)
    var_scale = scale * -var_weight * active / (feat * spread * (total - 1))
    cov_scale = scale * 4.0 * cov_weight / (feat * (total - 1)) / (total - 1)
    inv_scale = (1.0 - 2.0 * index) * scale * 2.0 * inv_weight / (total * feat)
    mean = sums[index : index + 1, :] / total
    norms = stats[index + 2 : index + 3, :]
    chunk = rows // 4
    for step in range(4):
        at = slice(step * chunk, (step + 1) * chunk)
        wide = grid[at, :].astype(jnp.float32)
        square_sum = square_sum + jnp.sum(wide * wide)
        product = dot(grid[at, :], rounded[index])
        product = product + (columns[at, 0:1] - norms) * rounded[
            index, at, :
        ].astype(jnp.float32)
        one, two = first[at, :].astype(jnp.float32), second[at, :].astype(jnp.float32)
        centred = (one if index == 0 else two) - mean
        base[at, :] = inv_scale * (one - two) + var_scale * centred + cov_scale * product
    squares[0] = square_sum


def far_product_kernel(x_count, total, feat, place, base, *rest):
    others, parts, grad = rest[:4], rest[4:-1], rest[-1]
    core, x_place = place[0], place[1]
    quarter = others[0].shape[0]
    half = 2 * quarter
    tile = half // x_count
    cov_scale = total * feat / 64.0 * 4.0 * cov_weight / (feat * (total - 1)) / (total - 1)
    for side in range(2):
        owner = core if side == 0 else 1 - core
        for step in range(x_count):
            at = (x_place + x_count - step) % x_count
            row = pl.ds(pl.multiple_of(half * owner + tile * at, tile), tile)
            product = jnp.zeros((tile, grad.shape[1]), jnp.float32)
            for block in range(2):
                part = parts[(block * 2 + side) * x_count + step]
                for index in range(2):
                    product = product + dot(
                        part[:tile, index * quarter : (index + 1) * quarter],
                        others[2 * block + index][...],
                    )
            grad[row, :] = base[row, :] + cov_scale * product


def squares_kernel(main, count, *refs):
    total = jnp.float32(0.0)
    terms = jnp.zeros((1, refs[0].shape[1]), jnp.float32)
    for ref in refs[:-2]:
        wide = ref[:main, :].astype(jnp.float32)
        total = total + jnp.sum(wide * wide)
        if ref.shape[0] > main:
            terms = terms + read_extra(ref, main)
    refs[-2][0] = total
    refs[-1][0] = jnp.sum(terms)


def on_device(first_view, second_view):
    dp_count = lax.axis_size("dp")
    row_count = lax.axis_size("row")
    col_count = lax.axis_size("col")
    rows, width = first_view.shape
    total = rows * dp_count
    feat = width * row_count * col_count
    half = rows // 2
    x_count = col_count // 2
    core = lax.axis_index("col") % 2
    x_place = lax.axis_index("col") // 2
    z_place = lax.axis_index("row")
    inner = 4 if row_count % 4 == 0 else 1
    middle = jnp.logical_or(z_place % 4 == 1, z_place % 4 == 2)
    place = jnp.stack([core, x_place, middle.astype(core.dtype)]).astype(jnp.int32)
    f32, bf16 = jnp.float32, jnp.bfloat16
    run = Chain()

    (sums,) = run(sums_kernel, [array((2, width), f32)], [first_view, second_view])
    sums_other = partner_of(sums, "dp", 1)
    first_sent, sums_other = lax.optimization_barrier((first_view, sums_other))
    others = [partner_of(first_sent, "dp", 1)]
    sums = sums + sums_other

    rounded, stats, second_sent = run(
        functools.partial(centre_kernel, total),
        [
            array((2, rows, width), bf16),
            array((8, width), f32),
            array((rows + 16, width), bf16),
        ],
        [first_view, second_view, sums],
    )
    others.append(partner_of(second_sent, "dp", 1))
    swapped = [
        [core_swap(rounded[view, :half]), core_swap(rounded[view, half:])] for view in range(2)
    ]

    def send_row(value, pairs):
        groups = range(0, row_count, inner)
        return lax.ppermute(value, "row", [(g + a, g + b) for g in groups for a, b in pairs])

    class Piece:
        def __init__(self, main, keep, sends):
            self.main, self.keep = main, keep
            self.like = array(keep.shape, bf16)
            self.got = [shift(sent, "col", x_count, i + 1, 2) for i, sent in enumerate(sends)]

        def add(self, values):
            (value,) = run(functools.partial(add_kernel, self.main), [self.like], values)
            return value

        def over_x(self):
            if inner == 4:
                value = self.add([self.keep] + self.got)
                self.got.append(send_row(value, [(0, 1), (3, 2)]))

        def inward(self):
            self.value = self.add([self.keep] + self.got)
            if inner == 4:
                self.got = send_row(self.value, [(1, 2), (2, 1)])

        def across(self):
            if inner == 4:
                self.value = self.add([self.value, self.got])
            bit = inner
            while bit < row_count:
                self.value = self.add([self.value, partner_of(self.value, "row", bit)])
                bit *= 2
            if inner == 4:
                self.got = send_row(self.value, [(1, 0), (2, 3)])

        def outward(self):
            if inner == 4:
                (self.value,) = run(pick_kernel, [self.like], [place, self.value, self.got])
            parts = [self.value]
            for step in range(1, x_count):
                parts.append(shift(self.value, "col", x_count, step, 2))
            self.parts = parts + [core_swap(part) for part in parts]

    near, far, rnd_others = [], [], []
    main = 3 * (rows // 4) // x_count
    tile = half // x_count

    def piece_outs(size):
        return [array((size, half), f32)] + [array((size, half), bf16)] * (x_count - 1)

    def near_gram(index):
        whole, *outs = run(
            functools.partial(near_kernel, x_count, index),
            [array((rows, width), bf16)] + piece_outs(main + 16),
            [place, rounded] + swapped[index],
        )
        swapped[index] = whole
        near.append(Piece(main, outs[0], outs[1:]))

    def far_centre(index):
        outs = [array((rows // 4, width), bf16)] * 4
        ins = [others[index], sums]
        if index == 1:
            outs, ins = outs + [array((8, width), f32)], ins + [stats]
        return run(functools.partial(centre_other_kernel, total, index), outs, ins)

    def far_gram(index, extra_ins):
        sizes = [tile + 16 * len(extra_ins), tile]
        outs = run(
            functools.partial(far_kernel, x_count, index, total, feat),
            piece_outs(sizes[0]) + piece_outs(sizes[1]),
            [place, rounded, swapped[index]]
            + rnd_others[index]
            + [core_swap(other) for other in rnd_others[index]]
            + extra_ins,
        )
        for block in range(2):
            keep, *sends = outs[block * x_count : (block + 1) * x_count]
            far.append(Piece(tile, keep, sends))

    def near_product(index):
        return run(
            functools.partial(near_product_kernel, x_count, index, total, feat),
            [array((rows, width), f32), array((1,), f32)],
            [place, rounded, first_view, second_view, sums, stats] + near[index].parts,
            scratch=[pltpu.VMEM((rows, rows), bf16), pltpu.VMEM((rows, 8), f32)],
        )

    def far_product(index, base):
        (grad,) = run(
            functools.partial(far_product_kernel, x_count, total, feat),
            [array((rows, width), f32)],
            [place, base]
            + rnd_others[index]
            + far[2 * index].parts
            + far[2 * index + 1].parts,
        )
        return grad

    near_gram(0)
    near_gram(1)
    near[0].over_x()
    rnd_others.append(list(far_centre(0)))
    far_gram(0, [])
    near[1].over_x()
    near[0].inward()
    far[0].over_x()
    far[1].over_x()
    near[1].inward()
    *found, stats = far_centre(1)
    rnd_others.append(found)
    near[0].across()
    far[0].inward()
    far_gram(1, [stats])
    far[1].inward()
    near[1].across()
    near[0].outward()
    far[0].across()
    far[2].over_x()
    far[1].across()
    far[3].over_x()
    near[1].outward()
    far[2].inward()
    far[0].outward()
    far[3].inward()
    far[1].outward()
    far[2].across()
    base_first, squares_first = near_product(0)
    base_second, squares_second = near_product(1)
    far[3].across()
    far[2].outward()
    grad_first = far_product(0, base_first)
    far[3].outward()
    squares_far, terms = run(
        functools.partial(squares_kernel, tile, x_count),
        [array((1,), f32), array((1,), f32)],
        [part for piece in far for part in piece.parts],
    )
    squares = squares_first[0] + squares_second[0] + squares_far[0]
    plane = squares / (total - 1) / (total - 1)
    plane_other = partner_of(plane, "dp", 1)
    grad_second = far_product(1, base_second)
    loss = terms[0] + cov_weight * (plane + plane_other) / feat
    return loss, grad_first, grad_second


def solution(mesh):
    return jax.shard_map(
        on_device,
        mesh=mesh,
        in_specs=(P("dp", ("row", "col")), P("dp", ("row", "col"))),
        out_specs=(P(), P("dp", ("row", "col")), P("dp", ("row", "col"))),
        check_vma=False,
    )
```

```python
import functools

import jax
import jax.numpy as jnp
from jax import lax
from jax.experimental import pallas as pl
from jax.experimental.pallas import tpu as pltpu
from jax.sharding import PartitionSpec as P

inv_weight = 25.0
var_weight = 25.0
cov_weight = 1.0
eps_var = 0.0001

ORDER = (
    "g0", "g1", "x0", "c0", "x1", "f0", "i0", "x2", "i1", "c1", "m0", "i2", "x3", "f1", "i3",
    "m1", "o0", "m2", "x4", "m3", "x5", "o1", "i4", "o2", "i5", "m4", "o3", "p0", "p1", "m5",
    "o4", "q2", "q3", "o5", "q4", "s5", "q5",
)

VMEM = pl.BlockSpec(memory_space=pltpu.VMEM)
SMEM = pl.BlockSpec(memory_space=pltpu.SMEM)
MIB = 1024 * 1024


class Chain:
    def __init__(self):
        self.last = None

    def __call__(self, kernel, outs, ins, scratch=(), extra=0):
        specs = [SMEM if x.ndim == 1 else VMEM for x in ins]
        body = kernel
        if self.last is not None:
            ins, specs = [self.last] + list(ins), [pl.BlockSpec(memory_space=pl.ANY)] + specs

            def body(_, *refs):
                kernel(*refs)

        size = sum(x.size * x.dtype.itemsize for x in list(ins) + list(outs)) + extra
        outs = pl.pallas_call(
            body,
            out_shape=outs,
            in_specs=specs,
            out_specs=[VMEM] * len(outs),
            scratch_shapes=scratch,
            compiler_params=pltpu.CompilerParams(vmem_limit_bytes=(size // MIB + 4) * MIB),
            cost_estimate=pl.CostEstimate(flops=1, bytes_accessed=1, transcendentals=0),
        )(*ins)
        self.last = outs[0]
        return outs


def array(shape, dtype):
    return jax.ShapeDtypeStruct(shape, dtype)


def shift(value, axis, count, step, inner):
    pairs = [
        (index, (index // inner + step) % count * inner + index % inner)
        for index in range(count * inner)
    ]
    return lax.ppermute(value, axis, pairs)


def partner_of(value, axis, bit):
    return lax.ppermute(value, axis, [(index, index ^ bit) for index in range(lax.axis_size(axis))])


def core_swap(value):
    return partner_of(value, "col", 1)


def dot_t(left, right):
    return lax.dot_general(
        left, right, (((1,), (1,)), ((), ())), preferred_element_type=jnp.float32
    )


def dot(left, right):
    return lax.dot_general(
        left, right, (((1,), (0,)), ((), ())), preferred_element_type=jnp.float32
    )


def sums_kernel(first, second, out):
    out[0:1, :] = jnp.sum(first[...].astype(jnp.float32), axis=0, keepdims=True)
    out[1:2, :] = jnp.sum(second[...].astype(jnp.float32), axis=0, keepdims=True)


def write_extra(out, main, extra):
    ids = lax.broadcasted_iota(jnp.int32, (16, extra.shape[1]), 0)
    if out.dtype == jnp.bfloat16:
        high = extra.astype(jnp.bfloat16).astype(jnp.float32)
        block = jnp.where(ids == 0, high, jnp.where(ids == 1, extra - high, 0.0))
    else:
        block = jnp.where(ids == 0, extra, 0.0)
    out[main : main + 16, :] = block.astype(out.dtype)


def read_extra(ref, main):
    block = ref[main : main + 16, :].astype(jnp.float32)
    return block[0:1, :] + block[1:2, :]


def centre_kernel(total, first, second, sums, stats, *pieces):
    width = first.shape[1]
    size = pieces[0].shape[0]
    found = []
    squares = []
    for index, view in enumerate((first, second)):
        mean = sums[index : index + 1, :] / total
        variance = jnp.zeros((1, width), jnp.float32)
        square = jnp.zeros((1, width), jnp.float32)
        for step in range(4):
            at = slice(step * size, (step + 1) * size)
            centred = view[at, :].astype(jnp.float32) - mean
            rounded = centred.astype(jnp.bfloat16)
            pieces[4 * index + step][...] = rounded
            wide = rounded.astype(jnp.float32)
            variance = variance + jnp.sum(centred * centred, axis=0, keepdims=True)
            square = square + jnp.sum(wide * wide, axis=0, keepdims=True)
        found.append(variance)
        squares.append(square)
    differ = first[...].astype(jnp.float32) - second[...].astype(jnp.float32)
    found += squares + [jnp.sum(differ * differ, axis=0, keepdims=True)]
    ids = lax.broadcasted_iota(jnp.int32, (8, width), 0)
    block = jnp.zeros((8, width), jnp.float32)
    for index, value in enumerate(found):
        block = jnp.where(ids == index, value, block)
    stats[...] = block


def near_place(tile_index, core, rows, tile):
    half, quarter = rows // 2, rows // 4
    square = tile_index < half // tile
    row = jnp.where(square, half * core + tile * tile_index, quarter * core + tile * tile_index - half)
    column = jnp.where(square, half * core, half)
    return square, pl.multiple_of(row, tile), pl.multiple_of(column, half)


def near_kernel(x_count, place, *rest):
    pieces, swapped, (own, partner, keep, *sends) = rest[:4], rest[4:8], rest[8:]
    core, x_place = place[0], place[1]
    rows = own.shape[0]
    half = rows // 2
    tile = rows // 4 // x_count
    for whole, parts in ((own, pieces), (partner, swapped)):
        for step, part in enumerate(parts):
            whole[step * (half // 2) : (step + 1) * (half // 2), :] = part[...]
    row_ids = lax.broadcasted_iota(jnp.int32, (tile, half), 0)
    column_ids = lax.broadcasted_iota(jnp.int32, (tile, half), 1)
    for step in range(x_count):
        out = keep if step == 0 else sends[step - 1]
        extra = jnp.zeros((1, half), jnp.float32)
        for piece in range(3):
            index = (x_place + step) % x_count * 3 + piece
            square, row, column = near_place(index, core, rows, tile)
            diagonal = jnp.logical_and(square, column_ids == row_ids + tile * index)
            value = dot_t(own[pl.ds(row, tile), :], own[pl.ds(column, half), :])
            value = value + dot_t(
                partner[pl.ds(row, tile), :], partner[pl.ds(column, half), :]
            )
            extra = extra + jnp.sum(jnp.where(diagonal, value, 0.0), axis=0, keepdims=True)
            value = jnp.where(diagonal, 0.0, value)
            out[pl.ds(piece * tile, tile), :] = value.astype(out.dtype)
        write_extra(out, 3 * tile, extra)


def centre_other_kernel(total, index, other, sums, *outs):
    mean = sums[index : index + 1, :] / total
    size = outs[0].shape[0]
    for step, out in enumerate(outs):
        at = slice(step * size, (step + 1) * size)
        out[...] = (other[at, :].astype(jnp.float32) - mean).astype(jnp.bfloat16)


def add_kernel(main, *refs):
    out = refs[-1]
    value = refs[0][:main, :].astype(jnp.float32)
    for ref in refs[1:-1]:
        value = value + ref[:main, :].astype(jnp.float32)
    out[:main, :] = value.astype(out.dtype)
    if main < out.shape[0]:
        extra = read_extra(refs[0], main)
        for ref in refs[1:-1]:
            extra = extra + read_extra(ref, main)
        write_extra(out, main, extra)


def pick_kernel(place, mine, got, out):
    @pl.when(place[2] == 1)
    def _():
        out[...] = mine[...]

    @pl.when(place[2] == 0)
    def _():
        out[...] = got[...]


def loss_terms(total, feat, stats):
    spread = jnp.sqrt(stats[0:2, :] / (total - 1) + eps_var)
    norms = stats[2:4, :] / (total - 1)
    return (
        inv_weight * stats[4:5, :] / (total * feat)
        + var_weight * jnp.sum(jnp.maximum(1.0 - spread, 0.0), axis=0, keepdims=True) / feat
        - cov_weight * jnp.sum(norms * norms, axis=0, keepdims=True) / feat
    )


def far_kernel(x_count, total, feat, place, own, partner, *rest):
    others, swapped, outs = rest[:4], rest[4:8], rest[8:]
    stats = None
    if len(outs) > 2 * x_count:
        stats, outs = outs[0], outs[1:]
    core, x_place = place[0], place[1]
    half = own.shape[0] // 2
    size = half // 2
    tile = half // x_count
    for block in range(2):
        for step in range(x_count):
            out = outs[block * x_count + step]
            part = (x_place + step) % x_count
            row = pl.ds(pl.multiple_of(half * core + tile * part, tile), tile)
            left, left_partner = own[row, :], partner[row, :]
            for side in range(2):
                at = 2 * block + side
                value = dot_t(left, others[at][...]) + dot_t(left_partner, swapped[at][...])
                out[:tile, side * size : (side + 1) * size] = value.astype(out.dtype)
            if out.shape[0] > tile:
                terms = loss_terms(total, feat, stats)
                terms = jnp.where(part == 0, terms, 0.0)
                if terms.shape[1] < half:
                    terms = jnp.concatenate(
                        [terms, jnp.zeros((1, half - terms.shape[1]), jnp.float32)], axis=1
                    )
                write_extra(out, tile, terms)


def near_product_kernel(
    x_count, index, total, feat, place, rounded, first, second, sums, stats, *rest
):
    parts, (base, squares, grid, columns) = rest[:-4], rest[-4:]
    core, x_place = place[0], place[1]
    rows, width = rounded.shape
    half = rows // 2
    tile = rows // 4 // x_count
    square_sum = jnp.zeros((1, half), jnp.float32)
    for side in range(2):
        owner = core if side == 0 else 1 - core
        extra = jnp.zeros((1, half), jnp.float32)
        for step in range(x_count):
            extra = extra + read_extra(parts[side * x_count + step], 3 * tile)
            for piece in range(3):
                at = (x_place + x_count - step) % x_count * 3 + piece
                _, row, column = near_place(at, owner, rows, tile)
                grid[pl.ds(row, tile), pl.ds(column, half)] = parts[side * x_count + step][
                    pl.ds(piece * tile, tile), :
                ]
        square_sum = square_sum + extra * extra
        columns[pl.ds(pl.multiple_of(half * owner, half), half), :] = jnp.broadcast_to(
            extra, (8, half)
        ).T
    grid[half:, :half] = grid[:half, half:].T
    scale = total * feat / 64.0
    spread = jnp.sqrt(stats[index : index + 1, :] / (total - 1) + eps_var)
    active = jnp.where(spread < 1.0, 1.0, 0.0)
    var_scale = scale * -var_weight * active / (feat * spread * (total - 1))
    cov_scale = scale * 4.0 * cov_weight / (feat * (total - 1)) / (total - 1)
    inv_scale = (1.0 - 2.0 * index) * scale * 2.0 * inv_weight / (total * feat)
    mean = sums[index : index + 1, :] / total
    norms = stats[index + 2 : index + 3, :]
    chunk = rows // 4
    for step in range(4):
        at = slice(step * chunk, (step + 1) * chunk)
        wide = grid[at, :].astype(jnp.float32)
        row = jnp.sum(wide * wide, axis=0, keepdims=True)
        square_sum = square_sum + row[:, :half] + row[:, half:]
        product = dot(grid[at, :], rounded[...])
        product = product + (columns[at, 0:1] - norms) * rounded[at, :].astype(
            jnp.float32
        )
        one, two = first[at, :].astype(jnp.float32), second[at, :].astype(jnp.float32)
        centred = (one if index == 0 else two) - mean
        base[at, :] = inv_scale * (one - two) + var_scale * centred + cov_scale * product
    squares[...] = square_sum


def far_product_kernel(x_count, total, feat, place, base, *rest):
    others, parts = rest[:2], rest[2 : 2 + 2 * x_count]
    grad, *sums = rest[2 + 2 * x_count :]
    core, x_place = place[0], place[1]
    size = others[0].shape[0]
    half = 2 * size
    tile = half // x_count
    cov_scale = total * feat / 64.0 * 4.0 * cov_weight / (feat * (total - 1)) / (total - 1)
    for side in range(2):
        owner = core if side == 0 else 1 - core
        for step in range(x_count):
            at = (x_place + x_count - step) % x_count
            row = pl.ds(pl.multiple_of(half * owner + tile * at, tile), tile)
            part = parts[side * x_count + step]
            product = jnp.zeros((tile, grad.shape[1]), jnp.float32)
            for index in range(2):
                product = product + dot(
                    part[:tile, index * size : (index + 1) * size], others[index][...]
                )
            grad[row, :] = base[row, :] + cov_scale * product
    if sums:
        add_squares(tile, parts, *sums)


def add_squares(main, parts, squares, terms):
    total = jnp.zeros((1, parts[0].shape[1]), jnp.float32)
    extra = jnp.zeros((1, parts[0].shape[1]), jnp.float32)
    for part in parts:
        wide = part[:main, :].astype(jnp.float32)
        total = total + jnp.sum(wide * wide, axis=0, keepdims=True)
        if part.shape[0] > main:
            extra = extra + read_extra(part, main)
    squares[...] = total
    terms[...] = extra


def squares_kernel(main, total, count, *refs):
    parts, (plane, terms) = refs[count:-2], refs[-2:]
    add_squares(main, parts, plane, terms)
    value = plane[...]
    for ref in refs[:count]:
        value = value + ref[...]
    plane[...] = value / (total - 1) / (total - 1)


def on_device(first_view, second_view):
    dp_count = lax.axis_size("dp")
    row_count = lax.axis_size("row")
    col_count = lax.axis_size("col")
    rows, width = first_view.shape
    total = rows * dp_count
    feat = width * row_count * col_count
    half = rows // 2
    x_count = col_count // 2
    core = lax.axis_index("col") % 2
    x_place = lax.axis_index("col") // 2
    z_place = lax.axis_index("row")
    inner = 4 if row_count % 4 == 0 else 1
    middle = jnp.logical_or(z_place % 4 == 1, z_place % 4 == 2)
    place = jnp.stack([core, x_place, middle.astype(core.dtype)]).astype(jnp.int32)
    f32, bf16 = jnp.float32, jnp.bfloat16
    run = Chain()

    (sums,) = run(sums_kernel, [array((2, width), f32)], [first_view, second_view])
    sums_other = partner_of(sums, "dp", 1)
    first_sent, second_sent, sums_other = lax.optimization_barrier(
        (first_view, second_view, sums_other)
    )
    others = [partner_of(first_sent, "dp", 1), partner_of(second_sent, "dp", 1)]
    sums = sums + sums_other

    stats, *rounded = run(
        functools.partial(centre_kernel, total),
        [array((8, width), f32)] + [array((rows // 4, width), bf16)] * 8,
        [first_view, second_view, sums],
    )
    swapped = [core_swap(piece) for piece in rounded]
    stats = stats + partner_of(stats, "dp", 1)

    def send_row(value, pairs):
        groups = range(0, row_count, inner)
        return lax.ppermute(value, "row", [(g + a, g + b) for g in groups for a, b in pairs])

    class Piece:
        def __init__(self, main, keep, sends):
            self.main, self.keep = main, keep
            self.like = array(keep.shape, bf16)
            self.got = [shift(sent, "col", x_count, i + 1, 2) for i, sent in enumerate(sends)]

        def add(self, values):
            (value,) = run(functools.partial(add_kernel, self.main), [self.like], values)
            return value

        def over_x(self):
            if inner == 4:
                value = self.add([self.keep] + self.got)
                self.got.append(send_row(value, [(0, 1), (3, 2)]))

        def inward(self):
            self.value = self.add([self.keep] + self.got)
            if inner == 4:
                self.got = send_row(self.value, [(1, 2), (2, 1)])

        def across(self):
            if inner == 4:
                self.value = self.add([self.value, self.got])
            bit = inner
            while bit < row_count:
                self.value = self.add([self.value, partner_of(self.value, "row", bit)])
                bit *= 2
            if inner == 4:
                self.got = send_row(self.value, [(1, 0), (2, 3)])

        def outward(self):
            if inner == 4:
                (self.value,) = run(pick_kernel, [self.like], [place, self.value, self.got])
            parts = [self.value]
            for step in range(1, x_count):
                parts.append(shift(self.value, "col", x_count, step, 2))
            self.parts = parts + [core_swap(part) for part in parts]

    main = 3 * (rows // 4) // x_count
    tile = half // x_count
    pieces, wholes, found, base, squares = {}, {}, {}, {}, []

    def piece_outs(size):
        return [array((size, half), f32)] + [array((size, half), bf16)] * (x_count - 1)

    def near_gram(index):
        at = slice(4 * index, 4 * index + 4)
        own, partner, *outs = run(
            functools.partial(near_kernel, x_count),
            [array((rows, width), bf16)] * 2 + piece_outs(main + 16),
            [place] + rounded[at] + swapped[at],
        )
        wholes[index] = [own, partner]
        pieces[index] = Piece(main, outs[0], outs[1:])

    def far_centre(index):
        outs = [array((rows // 4, width), bf16)] * 4
        ins = [others[index], sums]
        found[index] = list(run(functools.partial(centre_other_kernel, total, index), outs, ins))

    def far_gram(index):
        outs = run(
            functools.partial(far_kernel, x_count, total, feat),
            piece_outs(tile + 16 * index) + piece_outs(tile),
            [place]
            + wholes[index]
            + found[index]
            + [core_swap(other) for other in found[index]]
            + [stats] * index,
        )
        for block in range(2):
            keep, *sends = outs[block * x_count : (block + 1) * x_count]
            pieces[2 + 2 * index + block] = Piece(tile, keep, sends)

    def near_product(index):
        base[index], value = run(
            functools.partial(near_product_kernel, x_count, index, total, feat),
            [array((rows, width), f32), array((1, half), f32)],
            [place, wholes[index][0], first_view, second_view, sums, stats]
            + pieces[index].parts,
            scratch=[pltpu.VMEM((rows, rows), bf16), pltpu.VMEM((rows, 8), f32)],
            extra=2 * rows * rows + 512 * rows,
        )
        squares.append(value)

    def far_product(index):
        view, block = index // 2 - 1, index % 2
        outs = [array((rows, width), f32)]
        if index < 5:
            outs += [array((1, half), f32)] * 2
        base[view], *value = run(
            functools.partial(far_product_kernel, x_count, total, feat),
            outs,
            [place, base[view]] + found[view][2 * block : 2 * block + 2] + pieces[index].parts,
        )
        squares.extend(value[:1])
        if index == 4:
            found["terms"] = value[1]

    def last_squares(index):
        plane, _ = run(
            functools.partial(squares_kernel, tile, total, len(squares)),
            [array((1, half), f32)] * 2,
            squares + pieces[index].parts,
        )
        found["plane"] = plane + partner_of(plane, "dp", 1)

    steps = {
        "g": near_gram,
        "c": far_centre,
        "f": far_gram,
        "x": lambda index: pieces[index].over_x(),
        "i": lambda index: pieces[index].inward(),
        "m": lambda index: pieces[index].across(),
        "o": lambda index: pieces[index].outward(),
        "p": near_product,
        "q": far_product,
        "s": last_squares,
    }
    for step in ORDER:
        steps[step[0]](int(step[1]))
    loss = jnp.sum(found["terms"] + cov_weight * found["plane"] / feat)
    return loss, base[0], base[1]


def solution(mesh):
    return jax.shard_map(
        on_device,
        mesh=mesh,
        in_specs=(P("dp", ("row", "col")), P("dp", ("row", "col"))),
        out_specs=(P(), P("dp", ("row", "col")), P("dp", ("row", "col"))),
        check_vma=False,
    )
```

```python
import functools

import jax
import jax.numpy as jnp
from jax import lax
from jax.experimental import pallas as pl
from jax.experimental.pallas import tpu as pltpu
from jax.sharding import PartitionSpec as P

inv_weight = 25.0
var_weight = 25.0
cov_weight = 1.0
eps_var = 0.0001

ORDER = (
    "g0", "g1", "x0", "c0", "x1", "f0", "i0", "x2", "x3", "i1", "c1", "m0", "i2", "f1", "t5",
    "i3", "m1", "o0", "m2", "x4", "m3", "x5", "o1", "i4", "o2", "i5", "m4", "o3", "m5", "o4",
    "p0", "p1", "o5", "q2", "q3", "q4", "e5", "s5", "q5",
)

VMEM = pl.BlockSpec(memory_space=pltpu.VMEM)
MIB = 1024 * 1024


class Chain:
    def __init__(self):
        self.last = None

    def __call__(self, kernel, outs, ins, scratch=(), extra=0):
        specs = [VMEM] * len(ins)
        body = kernel
        if self.last is not None:
            ins, specs = [self.last] + list(ins), [pl.BlockSpec(memory_space=pl.ANY)] + specs

            def body(_, *refs):
                kernel(*refs)

        size = sum(x.size * x.dtype.itemsize for x in list(ins) + list(outs)) + extra
        outs = pl.pallas_call(
            body,
            out_shape=outs,
            in_specs=specs,
            out_specs=[VMEM] * len(outs),
            scratch_shapes=scratch,
            compiler_params=pltpu.CompilerParams(vmem_limit_bytes=(size // MIB + 4) * MIB),
            cost_estimate=pl.CostEstimate(flops=1, bytes_accessed=1, transcendentals=0),
        )(*ins)
        self.last = outs[0]
        return outs


def array(shape, dtype):
    return jax.ShapeDtypeStruct(shape, dtype)


def shift(value, axis, count, step, inner):
    pairs = [
        (index, (index // inner + step) % count * inner + index % inner)
        for index in range(count * inner)
    ]
    return lax.ppermute(value, axis, pairs)


def partner_of(value, axis, bit):
    return lax.ppermute(value, axis, [(index, index ^ bit) for index in range(lax.axis_size(axis))])


def core_swap(value):
    return partner_of(value, "col", 1)


def dot_t(left, right):
    return lax.dot_general(
        left, right, (((1,), (1,)), ((), ())), preferred_element_type=jnp.float32
    )


def dot(left, right):
    return lax.dot_general(
        left, right, (((1,), (0,)), ((), ())), preferred_element_type=jnp.float32
    )


def sums_kernel(first, second, out, held, sems):
    count = held.shape[0]
    size = held.shape[1]
    copies = []
    for at in range(count):
        view = (first, second)[at % 2]
        rows = view.at[pl.ds(at // 2 * size, size), :]
        copies.append(pltpu.make_async_copy(rows, held.at[at], sems.at[at]))
        copies[-1].start()
    totals = [jnp.zeros((1, held.shape[2]), jnp.float32)] * 2
    for at, copy in enumerate(copies):
        copy.wait()
        part = jnp.sum(held[at].astype(jnp.float32), axis=0, keepdims=True)
        totals[at % 2] = totals[at % 2] + part
    out[0:1, :] = totals[0]
    out[1:2, :] = totals[1]


def column_sums(first, second):
    rows, width = first.shape
    return pl.pallas_call(
        sums_kernel,
        out_shape=array((2, width), jnp.float32),
        in_specs=[pl.BlockSpec(memory_space=pl.ANY)] * 2,
        out_specs=VMEM,
        scratch_shapes=[
            pltpu.VMEM((8, rows // 4, width), jnp.bfloat16),
            pltpu.SemaphoreType.DMA((8,)),
        ],
        compiler_params=pltpu.CompilerParams(vmem_limit_bytes=8 * MIB),
        cost_estimate=pl.CostEstimate(flops=1, bytes_accessed=1, transcendentals=0),
    )(first, second)


def write_extra(out, main, extra):
    ids = lax.broadcasted_iota(jnp.int32, (16, extra.shape[1]), 0)
    if out.dtype == jnp.bfloat16:
        high = extra.astype(jnp.bfloat16).astype(jnp.float32)
        block = jnp.where(ids == 0, high, jnp.where(ids == 1, extra - high, 0.0))
    else:
        block = jnp.where(ids == 0, extra, 0.0)
    out[main : main + 16, :] = block.astype(out.dtype)


def read_extra(ref, main):
    block = ref[main : main + 16, :].astype(jnp.float32)
    return block[0:1, :] + block[1:2, :]


def centre_kernel(total, first, second, sums, stats, *pieces):
    width = first.shape[1]
    size = pieces[0].shape[0]
    found = []
    squares = []
    for index, view in enumerate((first, second)):
        mean = sums[index : index + 1, :] / total
        variance = jnp.zeros((1, width), jnp.float32)
        square = jnp.zeros((1, width), jnp.float32)
        for step in range(4):
            at = slice(step * size, (step + 1) * size)
            centred = view[at, :].astype(jnp.float32) - mean
            rounded = centred.astype(jnp.bfloat16)
            pieces[4 * index + step][...] = rounded
            wide = rounded.astype(jnp.float32)
            variance = variance + jnp.sum(centred * centred, axis=0, keepdims=True)
            square = square + jnp.sum(wide * wide, axis=0, keepdims=True)
        found.append(variance)
        squares.append(square)
    differ = first[...].astype(jnp.float32) - second[...].astype(jnp.float32)
    found += squares + [jnp.sum(differ * differ, axis=0, keepdims=True)]
    ids = lax.broadcasted_iota(jnp.int32, (8, width), 0)
    block = jnp.zeros((8, width), jnp.float32)
    for index, value in enumerate(found):
        block = jnp.where(ids == index, value, block)
    stats[...] = block


def whereabouts():
    core = lax.axis_index("col") % 2
    return core, lax.axis_index("col") // 2


def near_place(tile_index, core, rows, tile):
    half, quarter = rows // 2, rows // 4
    square = tile_index < half // tile
    row = jnp.where(square, half * core + tile * tile_index, quarter * core + tile * tile_index - half)
    column = jnp.where(square, half * core, half)
    return square, pl.multiple_of(row, tile), pl.multiple_of(column, half)


def near_kernel(x_count, *rest):
    pieces, swapped, (own, partner, keep, *sends) = rest[:4], rest[4:8], rest[8:]
    core, x_place = whereabouts()
    rows = own.shape[0]
    half = rows // 2
    tile = rows // 4 // x_count
    for whole, parts in ((own, pieces), (partner, swapped)):
        for step, part in enumerate(parts):
            whole[step * (half // 2) : (step + 1) * (half // 2), :] = part[...]
    row_ids = lax.broadcasted_iota(jnp.int32, (tile, half), 0)
    column_ids = lax.broadcasted_iota(jnp.int32, (tile, half), 1)
    for step in range(x_count):
        out = keep if step == 0 else sends[step - 1]
        extra = jnp.zeros((1, half), jnp.float32)
        for piece in range(3):
            index = (x_place + step) % x_count * 3 + piece
            square, row, column = near_place(index, core, rows, tile)
            diagonal = jnp.logical_and(square, column_ids == row_ids + tile * index)
            value = dot_t(own[pl.ds(row, tile), :], own[pl.ds(column, half), :])
            value = value + dot_t(
                partner[pl.ds(row, tile), :], partner[pl.ds(column, half), :]
            )
            extra = extra + jnp.sum(jnp.where(diagonal, value, 0.0), axis=0, keepdims=True)
            value = jnp.where(diagonal, 0.0, value)
            out[pl.ds(piece * tile, tile), :] = value.astype(out.dtype)
        write_extra(out, 3 * tile, extra)


def centre_other_kernel(total, index, other, sums, *outs):
    mean = sums[index : index + 1, :] / total
    size = outs[0].shape[0]
    for step, out in enumerate(outs):
        at = slice(step * size, (step + 1) * size)
        out[...] = (other[at, :].astype(jnp.float32) - mean).astype(jnp.bfloat16)


def add_kernel(main, *refs):
    ins, out = refs[:-1], refs[-1]
    values = [ref[:main, :].astype(jnp.float32) for ref in ins if ref.shape[0] > 1]
    out[:main, :] = sum(values[1:], values[0]).astype(out.dtype)
    if main < out.shape[0]:
        extras = [ref[...] for ref in ins if ref.shape[0] == 1]
        extras += [read_extra(ref, main) for ref in ins if ref.shape[0] > main]
        write_extra(out, main, sum(extras[1:], extras[0]))


def pick_kernel(mine, got, out):
    z_place = lax.axis_index("row") % 4
    middle = jnp.logical_or(z_place == 1, z_place == 2)

    @pl.when(middle)
    def _():
        out[...] = mine[...]

    @pl.when(jnp.logical_not(middle))
    def _():
        out[...] = got[...]


def stats_kernel(total, feat, stats, sums, first, second, stats_out, terms):
    width = first.shape[1]
    found = []
    squares = []
    for index, view in enumerate((first, second)):
        centred = view[...].astype(jnp.float32) - sums[index : index + 1, :] / total
        wide = centred.astype(jnp.bfloat16).astype(jnp.float32)
        found.append(jnp.sum(centred * centred, axis=0, keepdims=True))
        squares.append(jnp.sum(wide * wide, axis=0, keepdims=True))
    differ = first[...].astype(jnp.float32) - second[...].astype(jnp.float32)
    found += squares + [jnp.sum(differ * differ, axis=0, keepdims=True)]
    found = [value + stats[at : at + 1, :] for at, value in enumerate(found)]
    ids = lax.broadcasted_iota(jnp.int32, stats.shape, 0)
    block = jnp.zeros(stats.shape, jnp.float32)
    for index, value in enumerate(found):
        block = jnp.where(ids == index, value, block)
    stats_out[...] = block
    value = inv_weight * found[4] / (total * feat)
    for index in range(2):
        spread = jnp.sqrt(found[index] / (total - 1) + eps_var)
        norms = found[index + 2] / (total - 1)
        value = value + var_weight * jnp.maximum(1.0 - spread, 0.0) / feat
        value = value - cov_weight * norms * norms / feat
    if terms.shape[1] > width:
        value = jnp.concatenate(
            [value, jnp.zeros((1, terms.shape[1] - width), jnp.float32)], axis=1
        )
    terms[...] = value


def far_kernel(x_count, own, partner, *rest):
    others, swapped, outs = rest[:4], rest[4:8], rest[8:]
    core, x_place = whereabouts()
    half = own.shape[0] // 2
    size = half // 2
    tile = half // x_count
    for block in range(2):
        for step in range(x_count):
            out = outs[block * x_count + step]
            part = (x_place + step) % x_count
            row = pl.ds(pl.multiple_of(half * core + tile * part, tile), tile)
            left, left_partner = own[row, :], partner[row, :]
            for side in range(2):
                at = 2 * block + side
                value = dot_t(left, others[at][...]) + dot_t(left_partner, swapped[at][...])
                out[:tile, side * size : (side + 1) * size] = value.astype(out.dtype)


def near_product_kernel(
    x_count, index, total, feat, rounded, first, second, sums, stats, *rest
):
    parts, (base, squares, grid, columns) = rest[:-4], rest[-4:]
    core, x_place = whereabouts()
    rows, width = rounded.shape
    half = rows // 2
    tile = rows // 4 // x_count
    square_sum = jnp.zeros((1, half), jnp.float32)
    for side in range(2):
        owner = core if side == 0 else 1 - core
        extra = jnp.zeros((1, half), jnp.float32)
        for step in range(x_count):
            extra = extra + read_extra(parts[side * x_count + step], 3 * tile)
            for piece in range(3):
                at = (x_place + x_count - step) % x_count * 3 + piece
                _, row, column = near_place(at, owner, rows, tile)
                grid[pl.ds(row, tile), pl.ds(column, half)] = parts[side * x_count + step][
                    pl.ds(piece * tile, tile), :
                ]
        square_sum = square_sum + extra * extra
        columns[pl.ds(pl.multiple_of(half * owner, half), half), :] = jnp.broadcast_to(
            extra, (8, half)
        ).T
    grid[half:, :half] = grid[:half, half:].T
    scale = total * feat / 64.0
    spread = jnp.sqrt(stats[index : index + 1, :] / (total - 1) + eps_var)
    active = jnp.where(spread < 1.0, 1.0, 0.0)
    var_scale = scale * -var_weight * active / (feat * spread * (total - 1))
    cov_scale = scale * 4.0 * cov_weight / (feat * (total - 1)) / (total - 1)
    inv_scale = (1.0 - 2.0 * index) * scale * 2.0 * inv_weight / (total * feat)
    mean = sums[index : index + 1, :] / total
    norms = stats[index + 2 : index + 3, :]
    chunk = rows // 4
    for step in range(4):
        at = slice(step * chunk, (step + 1) * chunk)
        wide = grid[at, :].astype(jnp.float32)
        row = jnp.sum(wide * wide, axis=0, keepdims=True)
        square_sum = square_sum + row[:, :half] + row[:, half:]
        product = dot(grid[at, :], rounded[...])
        product = product + (columns[at, 0:1] - norms) * rounded[at, :].astype(
            jnp.float32
        )
        one, two = first[at, :].astype(jnp.float32), second[at, :].astype(jnp.float32)
        centred = (one if index == 0 else two) - mean
        base[at, :] = inv_scale * (one - two) + var_scale * centred + cov_scale * product
    squares[...] = square_sum


def far_product_kernel(x_count, total, feat, base, *rest):
    others, parts = rest[:2], rest[2 : 2 + 2 * x_count]
    grad, *sums = rest[2 + 2 * x_count :]
    core, x_place = whereabouts()
    size = others[0].shape[0]
    half = 2 * size
    tile = half // x_count
    cov_scale = total * feat / 64.0 * 4.0 * cov_weight / (feat * (total - 1)) / (total - 1)
    for side in range(2):
        owner = core if side == 0 else 1 - core
        for step in range(x_count):
            at = (x_place + x_count - step) % x_count
            row = pl.ds(pl.multiple_of(half * owner + tile * at, tile), tile)
            part = parts[side * x_count + step]
            product = jnp.zeros((tile, grad.shape[1]), jnp.float32)
            for index in range(2):
                product = product + dot(
                    part[:tile, index * size : (index + 1) * size], others[index][...]
                )
            grad[row, :] = base[row, :] + cov_scale * product
    if sums:
        add_squares(tile, parts, *sums)


def add_squares(main, parts, squares, terms):
    total = jnp.zeros((1, parts[0].shape[1]), jnp.float32)
    extra = jnp.zeros((1, parts[0].shape[1]), jnp.float32)
    for part in parts:
        wide = part[:main, :].astype(jnp.float32)
        total = total + jnp.sum(wide * wide, axis=0, keepdims=True)
        if part.shape[0] > main:
            extra = extra + read_extra(part, main)
    squares[...] = total
    terms[...] = extra


def squares_kernel(main, total, count, *refs):
    parts, (plane, terms) = refs[count:-2], refs[-2:]
    add_squares(main, parts, plane, terms)
    value = plane[...]
    for ref in refs[:count]:
        value = value + ref[...]
    plane[...] = value / (total - 1) / (total - 1)


def on_device(first_view, second_view):
    dp_count = lax.axis_size("dp")
    row_count = lax.axis_size("row")
    col_count = lax.axis_size("col")
    rows, width = first_view.shape
    total = rows * dp_count
    feat = width * row_count * col_count
    half = rows // 2
    x_count = col_count // 2
    inner = 4 if row_count % 4 == 0 else 1
    f32, bf16 = jnp.float32, jnp.bfloat16
    run = Chain()

    sums = column_sums(first_view, second_view)
    sums_other = partner_of(sums, "dp", 1)
    first_sent, second_sent, sums_other = lax.optimization_barrier(
        (first_view, second_view, sums_other)
    )
    others = [partner_of(first_sent, "dp", 1), partner_of(second_sent, "dp", 1)]
    sums = sums + sums_other

    stats, *rounded = run(
        functools.partial(centre_kernel, total),
        [array((8, width), f32)] + [array((rows // 4, width), bf16)] * 8,
        [first_view, second_view, sums],
    )
    swapped = [core_swap(piece) for piece in rounded]
    stats_all = []

    def send_row(value, pairs):
        groups = range(0, row_count, inner)
        return lax.ppermute(value, "row", [(g + a, g + b) for g in groups for a, b in pairs])

    class Piece:
        def __init__(self, main, keep, sends):
            self.main, self.keep, self.row = main, keep, []
            self.like = array(keep.shape, bf16)
            self.got = [shift(sent, "col", x_count, i + 1, 2) for i, sent in enumerate(sends)]

        def extra(self, row):
            self.row = row
            self.like = array((self.main + 16, half), bf16)

        def add(self, values):
            (value,) = run(functools.partial(add_kernel, self.main), [self.like], values)
            return value

        def over_x(self):
            if inner == 4:
                value = self.add([self.keep] + self.got + self.row)
                self.got.append(send_row(value, [(0, 1), (3, 2)]))

        def inward(self):
            self.value = self.add([self.keep] + self.got + self.row)
            if inner == 4:
                self.got = send_row(self.value, [(1, 2), (2, 1)])

        def across(self):
            if inner == 4:
                self.value = self.add([self.value, self.got])
            bit = inner
            while bit < row_count:
                self.value = self.add([self.value, partner_of(self.value, "row", bit)])
                bit *= 2
            if inner == 4:
                self.got = send_row(self.value, [(1, 0), (2, 3)])

        def outward(self):
            if inner == 4:
                (self.value,) = run(pick_kernel, [self.like], [self.value, self.got])
            parts = [self.value]
            for step in range(1, x_count):
                parts.append(shift(self.value, "col", x_count, step, 2))
            self.parts = parts + [core_swap(part) for part in parts]

        def swap_after(self, value):
            parts = self.parts[:x_count]
            *late, value = lax.optimization_barrier((*parts[1:], value))
            self.parts = self.parts[: x_count + 1] + [core_swap(part) for part in late]
            return value

    main = 3 * (rows // 4) // x_count
    tile = half // x_count
    pieces, wholes, found, base, squares = {}, {}, {}, {}, []

    def piece_outs(size):
        return [array((size, half), f32)] + [array((size, half), bf16)] * (x_count - 1)

    def near_gram(index):
        at = slice(4 * index, 4 * index + 4)
        own, partner, *outs = run(
            functools.partial(near_kernel, x_count),
            [array((rows, width), bf16)] * 2 + piece_outs(main + 16),
            rounded[at] + swapped[at],
        )
        wholes[index] = [own, partner]
        pieces[index] = Piece(main, outs[0], outs[1:])

    def far_centre(index):
        outs = [array((rows // 4, width), bf16)] * 4
        ins = [others[index], sums]
        found[index] = list(run(functools.partial(centre_other_kernel, total, index), outs, ins))

    def far_gram(index):
        outs = run(
            functools.partial(far_kernel, x_count),
            piece_outs(tile) * 2,
            wholes[index] + found[index] + [core_swap(other) for other in found[index]],
        )
        for block in range(2):
            keep, *sends = outs[block * x_count : (block + 1) * x_count]
            pieces[2 + 2 * index + block] = Piece(tile, keep, sends)

    def other_stats(index):
        outs = run(
            functools.partial(stats_kernel, total, feat),
            [array((8, width), f32), array((1, half), f32)],
            [stats, sums] + others,
        )
        stats_all.append(outs[0])
        pieces[index].extra([outs[1]])

    def near_product(index):
        base[index], value = run(
            functools.partial(near_product_kernel, x_count, index, total, feat),
            [array((rows, width), f32), array((1, half), f32)],
            [wholes[index][0], first_view, second_view, sums, stats_all[0]]
            + pieces[index].parts,
            scratch=[pltpu.VMEM((rows, rows), bf16), pltpu.VMEM((rows, 8), f32)],
            extra=2 * rows * rows + 512 * rows,
        )
        squares.append(value)

    def far_product(index):
        view, block = index // 2 - 1, index % 2
        outs = [array((rows, width), f32)]
        if index < 5:
            outs += [array((1, half), f32)] * 2
        base[view], *value = run(
            functools.partial(far_product_kernel, x_count, total, feat),
            outs,
            [base[view]] + found[view][2 * block : 2 * block + 2] + pieces[index].parts,
        )
        squares.extend(value[:1])

    def last_swap(index):
        base[1] = pieces[index].swap_after(base[1])

    def last_squares(index):
        plane, found["terms"] = run(
            functools.partial(squares_kernel, tile, total, len(squares)),
            [array((1, half), f32)] * 2,
            squares + pieces[index].parts,
        )
        found["plane"] = plane + partner_of(plane, "dp", 1)

    steps = {
        "g": near_gram,
        "c": far_centre,
        "f": far_gram,
        "x": lambda index: pieces[index].over_x(),
        "i": lambda index: pieces[index].inward(),
        "m": lambda index: pieces[index].across(),
        "o": lambda index: pieces[index].outward(),
        "p": near_product,
        "q": far_product,
        "s": last_squares,
        "t": other_stats,
        "e": last_swap,
    }
    for step in ORDER:
        steps[step[0]](int(step[1]))
    loss = jnp.sum(found["terms"] + cov_weight * found["plane"] / feat)
    return loss, base[0], base[1]


def solution(mesh):
    return jax.shard_map(
        on_device,
        mesh=mesh,
        in_specs=(P("dp", ("row", "col")), P("dp", ("row", "col"))),
        out_specs=(P(), P("dp", ("row", "col")), P("dp", ("row", "col"))),
        check_vma=False,
    )
```

```python
import functools

import jax
import jax.numpy as jnp
from jax import lax
from jax.experimental import pallas as pl
from jax.experimental.pallas import tpu as pltpu
from jax.sharding import PartitionSpec as P

inv_weight = 25.0
var_weight = 25.0
cov_weight = 1.0
eps_var = 0.0001

ORDER = (
    "g0", "g1", "x0", "c0", "x1", "i0", "f0", "x2", "x3", "i1", "c1", "m0", "i2", "f1", "t5",
    "m1", "i3", "o0", "m2", "x4", "m3", "x5", "o1", "i4", "i5", "m4", "o3", "o2", "o4", "m5",
    "p0", "p1", "o5", "q2", "q3", "q4", "e5", "s5", "q5",
)

VMEM = pl.BlockSpec(memory_space=pltpu.VMEM)
MIB = 1024 * 1024


class Chain:
    def __init__(self):
        self.last = None

    def __call__(self, kernel, outs, ins, scratch=(), extra=0):
        specs = [VMEM] * len(ins)
        body = kernel
        if self.last is not None:
            ins, specs = [self.last] + list(ins), [pl.BlockSpec(memory_space=pl.ANY)] + specs

            def body(_, *refs):
                kernel(*refs)

        size = sum(x.size * x.dtype.itemsize for x in list(ins) + list(outs)) + extra
        outs = pl.pallas_call(
            body,
            out_shape=outs,
            in_specs=specs,
            out_specs=[VMEM] * len(outs),
            scratch_shapes=scratch,
            compiler_params=pltpu.CompilerParams(vmem_limit_bytes=(size // MIB + 4) * MIB),
            cost_estimate=pl.CostEstimate(flops=1, bytes_accessed=1, transcendentals=0),
        )(*ins)
        self.last = outs[0]
        return outs


def array(shape, dtype):
    return jax.ShapeDtypeStruct(shape, dtype)


def shift(value, axis, count, step, inner):
    pairs = [
        (index, (index // inner + step) % count * inner + index % inner)
        for index in range(count * inner)
    ]
    return lax.ppermute(value, axis, pairs)


def partner_of(value, axis, bit):
    return lax.ppermute(value, axis, [(index, index ^ bit) for index in range(lax.axis_size(axis))])


def core_swap(value):
    return partner_of(value, "col", 1)


def dot_t(left, right):
    return lax.dot_general(
        left, right, (((1,), (1,)), ((), ())), preferred_element_type=jnp.float32
    )


def dot(left, right):
    return lax.dot_general(
        left, right, (((1,), (0,)), ((), ())), preferred_element_type=jnp.float32
    )


def sums_kernel(first, second, out, held, sems):
    count = held.shape[0]
    size = held.shape[1]
    copies = []
    for at in range(count):
        view = (first, second)[at % 2]
        rows = view.at[pl.ds(at // 2 * size, size), :]
        copies.append(pltpu.make_async_copy(rows, held.at[at], sems.at[at]))
        copies[-1].start()
    totals = [jnp.zeros((1, held.shape[2]), jnp.float32)] * 2
    for at, copy in enumerate(copies):
        copy.wait()
        part = jnp.sum(held[at].astype(jnp.float32), axis=0, keepdims=True)
        totals[at % 2] = totals[at % 2] + part
    out[0:1, :] = totals[0]
    out[1:2, :] = totals[1]


def column_sums(first, second):
    rows, width = first.shape
    return pl.pallas_call(
        sums_kernel,
        out_shape=array((2, width), jnp.float32),
        in_specs=[pl.BlockSpec(memory_space=pl.ANY)] * 2,
        out_specs=VMEM,
        scratch_shapes=[
            pltpu.VMEM((8, rows // 4, width), jnp.bfloat16),
            pltpu.SemaphoreType.DMA((8,)),
        ],
        compiler_params=pltpu.CompilerParams(vmem_limit_bytes=8 * MIB),
        cost_estimate=pl.CostEstimate(flops=1, bytes_accessed=1, transcendentals=0),
    )(first, second)


def write_extra(out, main, extra):
    ids = lax.broadcasted_iota(jnp.int32, (16, extra.shape[1]), 0)
    if out.dtype == jnp.bfloat16:
        high = extra.astype(jnp.bfloat16).astype(jnp.float32)
        block = jnp.where(ids == 0, high, jnp.where(ids == 1, extra - high, 0.0))
    else:
        block = jnp.where(ids == 0, extra, 0.0)
    out[main : main + 16, :] = block.astype(out.dtype)


def read_extra(ref, main):
    block = ref[main : main + 16, :].astype(jnp.float32)
    return block[0:1, :] + block[1:2, :]


def centre_kernel(total, first, second, sums, stats, *pieces):
    width = first.shape[1]
    size = pieces[0].shape[0]
    found = []
    squares = []
    for index, view in enumerate((first, second)):
        mean = sums[index : index + 1, :] / total
        variance = jnp.zeros((1, width), jnp.float32)
        square = jnp.zeros((1, width), jnp.float32)
        for step in range(4):
            at = slice(step * size, (step + 1) * size)
            centred = view[at, :].astype(jnp.float32) - mean
            rounded = centred.astype(jnp.bfloat16)
            pieces[4 * index + step][...] = rounded
            wide = rounded.astype(jnp.float32)
            variance = variance + jnp.sum(centred * centred, axis=0, keepdims=True)
            square = square + jnp.sum(wide * wide, axis=0, keepdims=True)
        found.append(variance)
        squares.append(square)
    differ = first[...].astype(jnp.float32) - second[...].astype(jnp.float32)
    found += squares + [jnp.sum(differ * differ, axis=0, keepdims=True)]
    ids = lax.broadcasted_iota(jnp.int32, (8, width), 0)
    block = jnp.zeros((8, width), jnp.float32)
    for index, value in enumerate(found):
        block = jnp.where(ids == index, value, block)
    stats[...] = block


def whereabouts():
    core = lax.axis_index("col") % 2
    return core, lax.axis_index("col") // 2


def near_place(tile_index, core, rows, tile):
    half, quarter = rows // 2, rows // 4
    square = tile_index < half // tile
    row = jnp.where(square, half * core + tile * tile_index, quarter * core + tile * tile_index - half)
    column = jnp.where(square, half * core, half)
    return square, pl.multiple_of(row, tile), pl.multiple_of(column, half)


def near_kernel(x_count, *rest):
    pieces, swapped, (own, partner, keep, *sends) = rest[:4], rest[4:8], rest[8:]
    core, x_place = whereabouts()
    rows = own.shape[0]
    half = rows // 2
    tile = rows // 4 // x_count
    for whole, parts in ((own, pieces), (partner, swapped)):
        for step, part in enumerate(parts):
            whole[step * (half // 2) : (step + 1) * (half // 2), :] = part[...]
    row_ids = lax.broadcasted_iota(jnp.int32, (tile, half), 0)
    column_ids = lax.broadcasted_iota(jnp.int32, (tile, half), 1)
    for step in range(x_count):
        out = keep if step == 0 else sends[step - 1]
        extra = jnp.zeros((1, half), jnp.float32)
        for piece in range(3):
            index = (x_place + step) % x_count * 3 + piece
            square, row, column = near_place(index, core, rows, tile)
            diagonal = jnp.logical_and(square, column_ids == row_ids + tile * index)
            value = dot_t(own[pl.ds(row, tile), :], own[pl.ds(column, half), :])
            value = value + dot_t(
                partner[pl.ds(row, tile), :], partner[pl.ds(column, half), :]
            )
            extra = extra + jnp.sum(jnp.where(diagonal, value, 0.0), axis=0, keepdims=True)
            value = jnp.where(diagonal, 0.0, value)
            out[pl.ds(piece * tile, tile), :] = value.astype(out.dtype)
        write_extra(out, 3 * tile, extra)


def centre_other_kernel(total, index, other, sums, *outs):
    mean = sums[index : index + 1, :] / total
    size = outs[0].shape[0]
    for step, out in enumerate(outs):
        at = slice(step * size, (step + 1) * size)
        out[...] = (other[at, :].astype(jnp.float32) - mean).astype(jnp.bfloat16)


def add_kernel(main, *refs):
    ins, out = refs[:-1], refs[-1]
    values = [ref[:main, :].astype(jnp.float32) for ref in ins if ref.shape[0] > 1]
    out[:main, :] = sum(values[1:], values[0]).astype(out.dtype)
    if main < out.shape[0]:
        extras = [ref[...] for ref in ins if ref.shape[0] == 1]
        extras += [read_extra(ref, main) for ref in ins if ref.shape[0] > main]
        write_extra(out, main, sum(extras[1:], extras[0]))


def pick_kernel(mine, got, out):
    z_place = lax.axis_index("row") % 4
    middle = jnp.logical_or(z_place == 1, z_place == 2)

    @pl.when(middle)
    def _():
        out[...] = mine[...]

    @pl.when(jnp.logical_not(middle))
    def _():
        out[...] = got[...]


def stats_kernel(total, feat, stats, sums, first, second, stats_out, terms):
    width = first.shape[1]
    found = []
    squares = []
    for index, view in enumerate((first, second)):
        centred = view[...].astype(jnp.float32) - sums[index : index + 1, :] / total
        wide = centred.astype(jnp.bfloat16).astype(jnp.float32)
        found.append(jnp.sum(centred * centred, axis=0, keepdims=True))
        squares.append(jnp.sum(wide * wide, axis=0, keepdims=True))
    differ = first[...].astype(jnp.float32) - second[...].astype(jnp.float32)
    found += squares + [jnp.sum(differ * differ, axis=0, keepdims=True)]
    found = [value + stats[at : at + 1, :] for at, value in enumerate(found)]
    ids = lax.broadcasted_iota(jnp.int32, stats.shape, 0)
    block = jnp.zeros(stats.shape, jnp.float32)
    for index, value in enumerate(found):
        block = jnp.where(ids == index, value, block)
    stats_out[...] = block
    value = inv_weight * found[4] / (total * feat)
    for index in range(2):
        spread = jnp.sqrt(found[index] / (total - 1) + eps_var)
        norms = found[index + 2] / (total - 1)
        value = value + var_weight * jnp.maximum(1.0 - spread, 0.0) / feat
        value = value - cov_weight * norms * norms / feat
    if terms.shape[1] > width:
        value = jnp.concatenate(
            [value, jnp.zeros((1, terms.shape[1] - width), jnp.float32)], axis=1
        )
    terms[...] = value


def far_kernel(x_count, own, partner, *rest):
    others, swapped, outs = rest[:4], rest[4:8], rest[8:]
    core, x_place = whereabouts()
    half = own.shape[0] // 2
    size = half // 2
    tile = half // x_count
    for block in range(2):
        for step in range(x_count):
            out = outs[block * x_count + step]
            part = (x_place + step) % x_count
            row = pl.ds(pl.multiple_of(half * core + tile * part, tile), tile)
            left, left_partner = own[row, :], partner[row, :]
            for side in range(2):
                at = 2 * block + side
                value = dot_t(left, others[at][...]) + dot_t(left_partner, swapped[at][...])
                out[:tile, side * size : (side + 1) * size] = value.astype(out.dtype)


def near_product_kernel(
    x_count, index, total, feat, rounded, first, second, sums, stats, *rest
):
    parts, (base, squares, grid, columns) = rest[:-4], rest[-4:]
    core, x_place = whereabouts()
    rows, width = rounded.shape
    half = rows // 2
    tile = rows // 4 // x_count
    square_sum = jnp.zeros((1, half), jnp.float32)
    for side in range(2):
        owner = core if side == 0 else 1 - core
        extra = jnp.zeros((1, half), jnp.float32)
        for step in range(x_count):
            extra = extra + read_extra(parts[side * x_count + step], 3 * tile)
            for piece in range(3):
                at = (x_place + x_count - step) % x_count * 3 + piece
                _, row, column = near_place(at, owner, rows, tile)
                grid[pl.ds(row, tile), pl.ds(column, half)] = parts[side * x_count + step][
                    pl.ds(piece * tile, tile), :
                ]
        square_sum = square_sum + extra * extra
        columns[pl.ds(pl.multiple_of(half * owner, half), half), :] = jnp.broadcast_to(
            extra, (8, half)
        ).T
    grid[half:, :half] = grid[:half, half:].T
    scale = total * feat / 64.0
    spread = jnp.sqrt(stats[index : index + 1, :] / (total - 1) + eps_var)
    active = jnp.where(spread < 1.0, 1.0, 0.0)
    var_scale = scale * -var_weight * active / (feat * spread * (total - 1))
    cov_scale = scale * 4.0 * cov_weight / (feat * (total - 1)) / (total - 1)
    inv_scale = (1.0 - 2.0 * index) * scale * 2.0 * inv_weight / (total * feat)
    mean = sums[index : index + 1, :] / total
    norms = stats[index + 2 : index + 3, :]
    chunk = rows // 4
    for step in range(4):
        at = slice(step * chunk, (step + 1) * chunk)
        wide = grid[at, :].astype(jnp.float32)
        row = jnp.sum(wide * wide, axis=0, keepdims=True)
        square_sum = square_sum + row[:, :half] + row[:, half:]
        product = dot(grid[at, :], rounded[...])
        product = product + (columns[at, 0:1] - norms) * rounded[at, :].astype(
            jnp.float32
        )
        one, two = first[at, :].astype(jnp.float32), second[at, :].astype(jnp.float32)
        centred = (one if index == 0 else two) - mean
        base[at, :] = inv_scale * (one - two) + var_scale * centred + cov_scale * product
    squares[...] = square_sum


def far_product_kernel(x_count, total, feat, base, *rest):
    others, parts = rest[:2], rest[2 : 2 + 2 * x_count]
    grad, *sums = rest[2 + 2 * x_count :]
    core, x_place = whereabouts()
    size = others[0].shape[0]
    half = 2 * size
    tile = half // x_count
    cov_scale = total * feat / 64.0 * 4.0 * cov_weight / (feat * (total - 1)) / (total - 1)
    for side in range(2):
        owner = core if side == 0 else 1 - core
        for step in range(x_count):
            at = (x_place + x_count - step) % x_count
            row = pl.ds(pl.multiple_of(half * owner + tile * at, tile), tile)
            part = parts[side * x_count + step]
            product = jnp.zeros((tile, grad.shape[1]), jnp.float32)
            for index in range(2):
                product = product + dot(
                    part[:tile, index * size : (index + 1) * size], others[index][...]
                )
            grad[row, :] = base[row, :] + cov_scale * product
    if sums:
        add_squares(tile, parts, *sums)


def add_squares(main, parts, squares, terms):
    total = jnp.zeros((1, parts[0].shape[1]), jnp.float32)
    extra = jnp.zeros((1, parts[0].shape[1]), jnp.float32)
    for part in parts:
        wide = part[:main, :].astype(jnp.float32)
        total = total + jnp.sum(wide * wide, axis=0, keepdims=True)
        if part.shape[0] > main:
            extra = extra + read_extra(part, main)
    squares[...] = total
    terms[...] = extra


def squares_kernel(main, total, count, *refs):
    parts, (plane, terms) = refs[count:-2], refs[-2:]
    add_squares(main, parts, plane, terms)
    value = plane[...]
    for ref in refs[:count]:
        value = value + ref[...]
    plane[...] = value / (total - 1) / (total - 1)


def on_device(first_view, second_view):
    dp_count = lax.axis_size("dp")
    row_count = lax.axis_size("row")
    col_count = lax.axis_size("col")
    rows, width = first_view.shape
    total = rows * dp_count
    feat = width * row_count * col_count
    half = rows // 2
    x_count = col_count // 2
    inner = 4 if row_count % 4 == 0 else 1
    f32, bf16 = jnp.float32, jnp.bfloat16
    run = Chain()

    sums = column_sums(first_view, second_view)
    sums_other = partner_of(sums, "dp", 1)
    first_sent, second_sent, sums_other = lax.optimization_barrier(
        (first_view, second_view, sums_other)
    )
    others = [partner_of(first_sent, "dp", 1), partner_of(second_sent, "dp", 1)]
    sums = sums + sums_other

    stats, *rounded = run(
        functools.partial(centre_kernel, total),
        [array((8, width), f32)] + [array((rows // 4, width), bf16)] * 8,
        [first_view, second_view, sums],
    )
    swapped = [core_swap(piece) for piece in rounded]
    stats_all = []

    def send_row(value, pairs):
        groups = range(0, row_count, inner)
        return lax.ppermute(value, "row", [(g + a, g + b) for g in groups for a, b in pairs])

    class Piece:
        def __init__(self, main, keep, sends):
            self.main, self.keep, self.row = main, keep, []
            self.like = array(keep.shape, bf16)
            self.got = [shift(sent, "col", x_count, i + 1, 2) for i, sent in enumerate(sends)]

        def extra(self, row):
            self.row = row
            self.like = array((self.main + 16, half), bf16)

        def add(self, values):
            (value,) = run(functools.partial(add_kernel, self.main), [self.like], values)
            return value

        def over_x(self):
            if inner == 4:
                value = self.add([self.keep] + self.got + self.row)
                self.got.append(send_row(value, [(0, 1), (3, 2)]))

        def inward(self):
            self.value = self.add([self.keep] + self.got + self.row)
            if inner == 4:
                self.got = send_row(self.value, [(1, 2), (2, 1)])

        def across(self):
            if inner == 4:
                self.value = self.add([self.value, self.got])
            bit = inner
            while bit < row_count:
                self.value = self.add([self.value, partner_of(self.value, "row", bit)])
                bit *= 2
            if inner == 4:
                self.got = send_row(self.value, [(1, 0), (2, 3)])

        def outward(self):
            if inner == 4:
                (self.value,) = run(pick_kernel, [self.like], [self.value, self.got])
            parts = [self.value]
            for step in range(1, x_count):
                parts.append(shift(self.value, "col", x_count, step, 2))
            self.parts = parts + [core_swap(part) for part in parts]

        def swap_after(self, value):
            parts = self.parts[:x_count]
            *late, value = lax.optimization_barrier((*parts[1:], value))
            self.parts = self.parts[: x_count + 1] + [core_swap(part) for part in late]
            return value

    main = 3 * (rows // 4) // x_count
    tile = half // x_count
    pieces, wholes, found, base, squares = {}, {}, {}, {}, []

    def piece_outs(size):
        return [array((size, half), f32)] + [array((size, half), bf16)] * (x_count - 1)

    def near_gram(index):
        at = slice(4 * index, 4 * index + 4)
        own, partner, *outs = run(
            functools.partial(near_kernel, x_count),
            [array((rows, width), bf16)] * 2 + piece_outs(main + 16),
            rounded[at] + swapped[at],
        )
        wholes[index] = [own, partner]
        pieces[index] = Piece(main, outs[0], outs[1:])

    def far_centre(index):
        outs = [array((rows // 4, width), bf16)] * 4
        ins = [others[index], sums]
        found[index] = list(run(functools.partial(centre_other_kernel, total, index), outs, ins))

    def far_gram(index):
        outs = run(
            functools.partial(far_kernel, x_count),
            piece_outs(tile) * 2,
            wholes[index] + found[index] + [core_swap(other) for other in found[index]],
        )
        for block in range(2):
            keep, *sends = outs[block * x_count : (block + 1) * x_count]
            pieces[2 + 2 * index + block] = Piece(tile, keep, sends)

    def other_stats(index):
        outs = run(
            functools.partial(stats_kernel, total, feat),
            [array((8, width), f32), array((1, half), f32)],
            [stats, sums] + others,
        )
        stats_all.append(outs[0])
        pieces[index].extra([outs[1]])

    def near_product(index):
        base[index], value = run(
            functools.partial(near_product_kernel, x_count, index, total, feat),
            [array((rows, width), f32), array((1, half), f32)],
            [wholes[index][0], first_view, second_view, sums, stats_all[0]]
            + pieces[index].parts,
            scratch=[pltpu.VMEM((rows, rows), bf16), pltpu.VMEM((rows, 8), f32)],
            extra=2 * rows * rows + 512 * rows,
        )
        squares.append(value)

    def far_product(index):
        view, block = index // 2 - 1, index % 2
        outs = [array((rows, width), f32)]
        if index < 5:
            outs += [array((1, half), f32)] * 2
        base[view], *value = run(
            functools.partial(far_product_kernel, x_count, total, feat),
            outs,
            [base[view]] + found[view][2 * block : 2 * block + 2] + pieces[index].parts,
        )
        squares.extend(value[:1])

    def last_swap(index):
        base[1] = pieces[index].swap_after(base[1])

    def last_squares(index):
        plane, found["terms"] = run(
            functools.partial(squares_kernel, tile, total, len(squares)),
            [array((1, half), f32)] * 2,
            squares + pieces[index].parts,
        )
        found["plane"] = plane + partner_of(plane, "dp", 1)

    steps = {
        "g": near_gram,
        "c": far_centre,
        "f": far_gram,
        "x": lambda index: pieces[index].over_x(),
        "i": lambda index: pieces[index].inward(),
        "m": lambda index: pieces[index].across(),
        "o": lambda index: pieces[index].outward(),
        "p": near_product,
        "q": far_product,
        "s": last_squares,
        "t": other_stats,
        "e": last_swap,
    }
    for step in ORDER:
        steps[step[0]](int(step[1]))
    loss = jnp.sum(found["terms"] + cov_weight * found["plane"] / feat)
    return loss, base[0], base[1]


def solution(mesh):
    return jax.shard_map(
        on_device,
        mesh=mesh,
        in_specs=(P("dp", ("row", "col")), P("dp", ("row", "col"))),
        out_specs=(P(), P("dp", ("row", "col")), P("dp", ("row", "col"))),
        check_vma=False,
    )
```

```python
import functools

import jax
import jax.numpy as jnp
from jax import lax
from jax.experimental import pallas as pl
from jax.experimental.pallas import tpu as pltpu
from jax.sharding import PartitionSpec as P

inv_weight = 25.0
var_weight = 25.0
cov_weight = 1.0
eps_var = 0.0001

ORDER = (
    "g0", "g1", "x0", "c0", "x1", "i0", "f0", "x2", "x3", "i1", "c1", "m0", "i2", "f1", "t5",
    "m1", "i3", "o0", "m2", "x4", "m3", "x5", "o1", "i4", "i5", "m4", "o3", "o2", "o4", "m5",
    "p0", "p1", "o5", "q2", "q3", "q4", "e5", "s5", "q5",
)

VMEM = pl.BlockSpec(memory_space=pltpu.VMEM)
MIB = 1024 * 1024


class Chain:
    def __init__(self):
        self.last = None

    def __call__(self, kernel, outs, ins, scratch=(), extra=0):
        specs = [VMEM] * len(ins)
        body = kernel
        if self.last is not None:
            ins, specs = [self.last] + list(ins), [pl.BlockSpec(memory_space=pl.ANY)] + specs

            def body(_, *refs):
                kernel(*refs)

        size = sum(x.size * x.dtype.itemsize for x in list(ins) + list(outs)) + extra
        outs = pl.pallas_call(
            body,
            out_shape=outs,
            in_specs=specs,
            out_specs=[VMEM] * len(outs),
            scratch_shapes=scratch,
            compiler_params=pltpu.CompilerParams(vmem_limit_bytes=(size // MIB + 2) * MIB),
            cost_estimate=pl.CostEstimate(flops=1, bytes_accessed=1, transcendentals=0),
        )(*ins)
        self.last = outs[0]
        return outs


def array(shape, dtype):
    return jax.ShapeDtypeStruct(shape, dtype)


def shift(value, axis, count, step, inner):
    pairs = [
        (index, (index // inner + step) % count * inner + index % inner)
        for index in range(count * inner)
    ]
    return lax.ppermute(value, axis, pairs)


def partner_of(value, axis, bit):
    return lax.ppermute(value, axis, [(index, index ^ bit) for index in range(lax.axis_size(axis))])


def core_swap(value):
    return partner_of(value, "col", 1)


def dot_t(left, right):
    return lax.dot_general(
        left, right, (((1,), (1,)), ((), ())), preferred_element_type=jnp.float32
    )


def dot(left, right):
    return lax.dot_general(
        left, right, (((1,), (0,)), ((), ())), preferred_element_type=jnp.float32
    )


def sums_kernel(first, second, out, held, sems):
    count = held.shape[0]
    size = held.shape[1]
    copies = []
    for at in range(count):
        view = (first, second)[at % 2]
        rows = view.at[pl.ds(at // 2 * size, size), :]
        copies.append(pltpu.make_async_copy(rows, held.at[at], sems.at[at]))
        copies[-1].start()
    totals = [jnp.zeros((1, held.shape[2]), jnp.float32)] * 2
    for at, copy in enumerate(copies):
        copy.wait()
        part = jnp.sum(held[at].astype(jnp.float32), axis=0, keepdims=True)
        totals[at % 2] = totals[at % 2] + part
    out[0:1, :] = totals[0]
    out[1:2, :] = totals[1]


def column_sums(first, second):
    rows, width = first.shape
    return pl.pallas_call(
        sums_kernel,
        out_shape=array((2, width), jnp.float32),
        in_specs=[pl.BlockSpec(memory_space=pl.ANY)] * 2,
        out_specs=VMEM,
        scratch_shapes=[
            pltpu.VMEM((8, rows // 4, width), jnp.bfloat16),
            pltpu.SemaphoreType.DMA((8,)),
        ],
        compiler_params=pltpu.CompilerParams(vmem_limit_bytes=8 * MIB),
        cost_estimate=pl.CostEstimate(flops=1, bytes_accessed=1, transcendentals=0),
    )(first, second)


def write_extra(out, main, extra):
    ids = lax.broadcasted_iota(jnp.int32, (16, extra.shape[1]), 0)
    if out.dtype == jnp.bfloat16:
        high = extra.astype(jnp.bfloat16).astype(jnp.float32)
        block = jnp.where(ids == 0, high, jnp.where(ids == 1, extra - high, 0.0))
    else:
        block = jnp.where(ids == 0, extra, 0.0)
    out[main : main + 16, :] = block.astype(out.dtype)


def read_extra(ref, main):
    block = ref[main : main + 16, :].astype(jnp.float32)
    return block[0:1, :] + block[1:2, :]


def centre_kernel(total, first, second, sums, stats, *pieces):
    width = first.shape[1]
    size = pieces[0].shape[0]
    found = []
    squares = []
    for index, view in enumerate((first, second)):
        mean = sums[index : index + 1, :] / total
        variance = jnp.zeros((1, width), jnp.float32)
        square = jnp.zeros((1, width), jnp.float32)
        for step in range(4):
            at = slice(step * size, (step + 1) * size)
            centred = view[at, :].astype(jnp.float32) - mean
            rounded = centred.astype(jnp.bfloat16)
            pieces[4 * index + step][...] = rounded
            wide = rounded.astype(jnp.float32)
            variance = variance + jnp.sum(centred * centred, axis=0, keepdims=True)
            square = square + jnp.sum(wide * wide, axis=0, keepdims=True)
        found.append(variance)
        squares.append(square)
    differ = first[...].astype(jnp.float32) - second[...].astype(jnp.float32)
    found += squares + [jnp.sum(differ * differ, axis=0, keepdims=True)]
    ids = lax.broadcasted_iota(jnp.int32, (8, width), 0)
    block = jnp.zeros((8, width), jnp.float32)
    for index, value in enumerate(found):
        block = jnp.where(ids == index, value, block)
    stats[...] = block


def whereabouts():
    core = lax.axis_index("col") % 2
    return core, lax.axis_index("col") // 2


def near_place(tile_index, core, rows, tile):
    half, quarter = rows // 2, rows // 4
    square = tile_index < half // tile
    row = jnp.where(square, half * core + tile * tile_index, quarter * core + tile * tile_index - half)
    column = jnp.where(square, half * core, half)
    return square, pl.multiple_of(row, tile), pl.multiple_of(column, half)


def near_kernel(x_count, *rest):
    pieces, swapped, (own, partner, keep, *sends) = rest[:4], rest[4:8], rest[8:]
    core, x_place = whereabouts()
    rows = own.shape[0]
    half = rows // 2
    tile = rows // 4 // x_count
    for whole, parts in ((own, pieces), (partner, swapped)):
        for step, part in enumerate(parts):
            whole[step * (half // 2) : (step + 1) * (half // 2), :] = part[...]
    row_ids = lax.broadcasted_iota(jnp.int32, (tile, half), 0)
    column_ids = lax.broadcasted_iota(jnp.int32, (tile, half), 1)
    for step in range(x_count):
        out = keep if step == 0 else sends[step - 1]
        extra = jnp.zeros((1, half), jnp.float32)
        for piece in range(3):
            index = (x_place + step) % x_count * 3 + piece
            square, row, column = near_place(index, core, rows, tile)
            diagonal = jnp.logical_and(square, column_ids == row_ids + tile * index)
            value = dot_t(own[pl.ds(row, tile), :], own[pl.ds(column, half), :])
            value = value + dot_t(
                partner[pl.ds(row, tile), :], partner[pl.ds(column, half), :]
            )
            extra = extra + jnp.sum(jnp.where(diagonal, value, 0.0), axis=0, keepdims=True)
            value = jnp.where(diagonal, 0.0, value)
            out[pl.ds(piece * tile, tile), :] = value.astype(out.dtype)
        write_extra(out, 3 * tile, extra)


def centre_other_kernel(total, index, other, sums, *outs):
    mean = sums[index : index + 1, :] / total
    size = outs[0].shape[0]
    for step, out in enumerate(outs):
        at = slice(step * size, (step + 1) * size)
        out[...] = (other[at, :].astype(jnp.float32) - mean).astype(jnp.bfloat16)


def add_kernel(main, *refs):
    ins, out = refs[:-1], refs[-1]
    values = [ref[:main, :].astype(jnp.float32) for ref in ins if ref.shape[0] > 1]
    out[:main, :] = sum(values[1:], values[0]).astype(out.dtype)
    if main < out.shape[0]:
        extras = [ref[...] for ref in ins if ref.shape[0] == 1]
        extras += [read_extra(ref, main) for ref in ins if ref.shape[0] > main]
        write_extra(out, main, sum(extras[1:], extras[0]))


def pick_kernel(mine, got, out):
    z_place = lax.axis_index("row") % 4
    middle = jnp.logical_or(z_place == 1, z_place == 2)

    @pl.when(middle)
    def _():
        out[...] = mine[...]

    @pl.when(jnp.logical_not(middle))
    def _():
        out[...] = got[...]


def stats_kernel(total, feat, stats, sums, first, second, stats_out, terms):
    width = first.shape[1]
    found = []
    squares = []
    for index, view in enumerate((first, second)):
        centred = view[...].astype(jnp.float32) - sums[index : index + 1, :] / total
        wide = centred.astype(jnp.bfloat16).astype(jnp.float32)
        found.append(jnp.sum(centred * centred, axis=0, keepdims=True))
        squares.append(jnp.sum(wide * wide, axis=0, keepdims=True))
    differ = first[...].astype(jnp.float32) - second[...].astype(jnp.float32)
    found += squares + [jnp.sum(differ * differ, axis=0, keepdims=True)]
    found = [value + stats[at : at + 1, :] for at, value in enumerate(found)]
    ids = lax.broadcasted_iota(jnp.int32, stats.shape, 0)
    block = jnp.zeros(stats.shape, jnp.float32)
    for index, value in enumerate(found):
        block = jnp.where(ids == index, value, block)
    stats_out[...] = block
    value = inv_weight * found[4] / (total * feat)
    for index in range(2):
        spread = jnp.sqrt(found[index] / (total - 1) + eps_var)
        norms = found[index + 2] / (total - 1)
        value = value + var_weight * jnp.maximum(1.0 - spread, 0.0) / feat
        value = value - cov_weight * norms * norms / feat
    if terms.shape[1] > width:
        value = jnp.concatenate(
            [value, jnp.zeros((1, terms.shape[1] - width), jnp.float32)], axis=1
        )
    terms[...] = value


def far_kernel(x_count, own, partner, *rest):
    others, swapped, outs = rest[:4], rest[4:8], rest[8:]
    core, x_place = whereabouts()
    half = own.shape[0] // 2
    size = half // 2
    tile = half // x_count
    for block in range(2):
        for step in range(x_count):
            out = outs[block * x_count + step]
            part = (x_place + step) % x_count
            row = pl.ds(pl.multiple_of(half * core + tile * part, tile), tile)
            left, left_partner = own[row, :], partner[row, :]
            for side in range(2):
                at = 2 * block + side
                value = dot_t(left, others[at][...]) + dot_t(left_partner, swapped[at][...])
                out[:tile, side * size : (side + 1) * size] = value.astype(out.dtype)


def near_product_kernel(
    x_count, index, total, feat, rounded, first, second, sums, stats, *rest
):
    parts, (base, squares, grid, columns) = rest[:-4], rest[-4:]
    core, x_place = whereabouts()
    rows, width = rounded.shape
    half = rows // 2
    tile = rows // 4 // x_count
    square_sum = jnp.zeros((1, half), jnp.float32)
    for side in range(2):
        owner = core if side == 0 else 1 - core
        extra = jnp.zeros((1, half), jnp.float32)
        for step in range(x_count):
            extra = extra + read_extra(parts[side * x_count + step], 3 * tile)
            for piece in range(3):
                at = (x_place + x_count - step) % x_count * 3 + piece
                _, row, column = near_place(at, owner, rows, tile)
                grid[pl.ds(row, tile), pl.ds(column, half)] = parts[side * x_count + step][
                    pl.ds(piece * tile, tile), :
                ]
        square_sum = square_sum + extra * extra
        columns[pl.ds(pl.multiple_of(half * owner, half), half), :] = jnp.broadcast_to(
            extra, (8, half)
        ).T
    grid[half:, :half] = grid[:half, half:].T
    scale = total * feat / 64.0
    spread = jnp.sqrt(stats[index : index + 1, :] / (total - 1) + eps_var)
    active = jnp.where(spread < 1.0, 1.0, 0.0)
    var_scale = scale * -var_weight * active / (feat * spread * (total - 1))
    cov_scale = scale * 4.0 * cov_weight / (feat * (total - 1)) / (total - 1)
    inv_scale = (1.0 - 2.0 * index) * scale * 2.0 * inv_weight / (total * feat)
    mean = sums[index : index + 1, :] / total
    norms = stats[index + 2 : index + 3, :]
    chunk = rows // 4
    for step in range(4):
        at = slice(step * chunk, (step + 1) * chunk)
        wide = grid[at, :].astype(jnp.float32)
        row = jnp.sum(wide * wide, axis=0, keepdims=True)
        square_sum = square_sum + row[:, :half] + row[:, half:]
        product = dot(grid[at, :], rounded[...])
        product = product + (columns[at, 0:1] - norms) * rounded[at, :].astype(
            jnp.float32
        )
        one, two = first[at, :].astype(jnp.float32), second[at, :].astype(jnp.float32)
        centred = (one if index == 0 else two) - mean
        base[at, :] = inv_scale * (one - two) + var_scale * centred + cov_scale * product
    squares[...] = square_sum


def far_product_kernel(x_count, total, feat, base, *rest):
    others, parts = rest[:2], rest[2 : 2 + 2 * x_count]
    grad, *sums = rest[2 + 2 * x_count :]
    core, x_place = whereabouts()
    size = others[0].shape[0]
    half = 2 * size
    tile = half // x_count
    cov_scale = total * feat / 64.0 * 4.0 * cov_weight / (feat * (total - 1)) / (total - 1)
    for side in range(2):
        owner = core if side == 0 else 1 - core
        for step in range(x_count):
            at = (x_place + x_count - step) % x_count
            row = pl.ds(pl.multiple_of(half * owner + tile * at, tile), tile)
            part = parts[side * x_count + step]
            product = jnp.zeros((tile, grad.shape[1]), jnp.float32)
            for index in range(2):
                product = product + dot(
                    part[:tile, index * size : (index + 1) * size], others[index][...]
                )
            grad[row, :] = base[row, :] + cov_scale * product
    if sums:
        add_squares(tile, parts, *sums)


def add_squares(main, parts, squares, terms):
    total = jnp.zeros((1, parts[0].shape[1]), jnp.float32)
    extra = jnp.zeros((1, parts[0].shape[1]), jnp.float32)
    for part in parts:
        wide = part[:main, :].astype(jnp.float32)
        total = total + jnp.sum(wide * wide, axis=0, keepdims=True)
        if part.shape[0] > main:
            extra = extra + read_extra(part, main)
    squares[...] = total
    terms[...] = extra


def squares_kernel(main, total, count, *refs):
    parts, (plane, terms) = refs[count:-2], refs[-2:]
    add_squares(main, parts, plane, terms)
    value = plane[...]
    for ref in refs[:count]:
        value = value + ref[...]
    plane[...] = value / (total - 1) / (total - 1)


def on_device(first_view, second_view):
    dp_count = lax.axis_size("dp")
    row_count = lax.axis_size("row")
    col_count = lax.axis_size("col")
    rows, width = first_view.shape
    total = rows * dp_count
    feat = width * row_count * col_count
    half = rows // 2
    x_count = col_count // 2
    inner = 4 if row_count % 4 == 0 else 1
    f32, bf16 = jnp.float32, jnp.bfloat16
    run = Chain()

    sums = column_sums(first_view, second_view)
    sums_other = partner_of(sums, "dp", 1)
    first_sent, second_sent, sums_other = lax.optimization_barrier(
        (first_view, second_view, sums_other)
    )
    others = [partner_of(first_sent, "dp", 1), partner_of(second_sent, "dp", 1)]
    sums = sums + sums_other

    stats, *rounded = run(
        functools.partial(centre_kernel, total),
        [array((8, width), f32)] + [array((rows // 4, width), bf16)] * 8,
        [first_view, second_view, sums],
    )
    swapped = [core_swap(piece) for piece in rounded]
    stats_all = []

    def send_row(value, pairs):
        groups = range(0, row_count, inner)
        return lax.ppermute(value, "row", [(g + a, g + b) for g in groups for a, b in pairs])

    class Piece:
        def __init__(self, main, keep, sends):
            self.main, self.keep, self.row = main, keep, []
            self.like = array(keep.shape, bf16)
            self.got = [shift(sent, "col", x_count, i + 1, 2) for i, sent in enumerate(sends)]

        def extra(self, row):
            self.row = row
            self.like = array((self.main + 16, half), bf16)

        def add(self, values):
            (value,) = run(functools.partial(add_kernel, self.main), [self.like], values)
            return value

        def over_x(self):
            if inner == 4:
                value = self.add([self.keep] + self.got + self.row)
                self.got.append(send_row(value, [(0, 1), (3, 2)]))

        def inward(self):
            self.value = self.add([self.keep] + self.got + self.row)
            if inner == 4:
                self.got = send_row(self.value, [(1, 2), (2, 1)])

        def across(self):
            if inner == 4:
                self.value = self.add([self.value, self.got])
            bit = inner
            while bit < row_count:
                self.value = self.add([self.value, partner_of(self.value, "row", bit)])
                bit *= 2
            if inner == 4:
                self.got = send_row(self.value, [(1, 0), (2, 3)])

        def outward(self):
            if inner == 4:
                (self.value,) = run(pick_kernel, [self.like], [self.value, self.got])
            parts = [self.value]
            for step in range(1, x_count):
                parts.append(shift(self.value, "col", x_count, step, 2))
            self.parts = parts + [core_swap(part) for part in parts]

        def swap_after(self, value):
            parts = self.parts[:x_count]
            *late, value = lax.optimization_barrier((*parts[1:], value))
            self.parts = self.parts[: x_count + 1] + [core_swap(part) for part in late]
            return value

    main = 3 * (rows // 4) // x_count
    tile = half // x_count
    pieces, wholes, found, base, squares = {}, {}, {}, {}, []

    def piece_outs(size):
        return [array((size, half), f32)] + [array((size, half), bf16)] * (x_count - 1)

    def near_gram(index):
        at = slice(4 * index, 4 * index + 4)
        own, partner, *outs = run(
            functools.partial(near_kernel, x_count),
            [array((rows, width), bf16)] * 2 + piece_outs(main + 16),
            rounded[at] + swapped[at],
        )
        wholes[index] = [own, partner]
        pieces[index] = Piece(main, outs[0], outs[1:])

    def far_centre(index):
        outs = [array((rows // 4, width), bf16)] * 4
        ins = [others[index], sums]
        found[index] = list(run(functools.partial(centre_other_kernel, total, index), outs, ins))

    def far_gram(index):
        outs = run(
            functools.partial(far_kernel, x_count),
            piece_outs(tile) * 2,
            wholes[index] + found[index] + [core_swap(other) for other in found[index]],
        )
        for block in range(2):
            keep, *sends = outs[block * x_count : (block + 1) * x_count]
            pieces[2 + 2 * index + block] = Piece(tile, keep, sends)

    def other_stats(index):
        outs = run(
            functools.partial(stats_kernel, total, feat),
            [array((8, width), f32), array((1, half), f32)],
            [stats, sums] + others,
        )
        stats_all.append(outs[0])
        pieces[index].extra([outs[1]])

    def near_product(index):
        base[index], value = run(
            functools.partial(near_product_kernel, x_count, index, total, feat),
            [array((rows, width), f32), array((1, half), f32)],
            [wholes[index][0], first_view, second_view, sums, stats_all[0]]
            + pieces[index].parts,
            scratch=[pltpu.VMEM((rows, rows), bf16), pltpu.VMEM((rows, 8), f32)],
            extra=2 * rows * rows + 512 * rows,
        )
        squares.append(value)

    def far_product(index):
        view, block = index // 2 - 1, index % 2
        outs = [array((rows, width), f32)]
        if index < 5:
            outs += [array((1, half), f32)] * 2
        base[view], *value = run(
            functools.partial(far_product_kernel, x_count, total, feat),
            outs,
            [base[view]] + found[view][2 * block : 2 * block + 2] + pieces[index].parts,
        )
        squares.extend(value[:1])

    def last_swap(index):
        base[1] = pieces[index].swap_after(base[1])

    def last_squares(index):
        plane, found["terms"] = run(
            functools.partial(squares_kernel, tile, total, len(squares)),
            [array((1, half), f32)] * 2,
            squares + pieces[index].parts,
        )
        found["plane"] = plane + partner_of(plane, "dp", 1)

    steps = {
        "g": near_gram,
        "c": far_centre,
        "f": far_gram,
        "x": lambda index: pieces[index].over_x(),
        "i": lambda index: pieces[index].inward(),
        "m": lambda index: pieces[index].across(),
        "o": lambda index: pieces[index].outward(),
        "p": near_product,
        "q": far_product,
        "s": last_squares,
        "t": other_stats,
        "e": last_swap,
    }
    for step in ORDER:
        steps[step[0]](int(step[1]))
    loss = jnp.sum(found["terms"] + cov_weight * found["plane"] / feat)
    return loss, base[0], base[1]


def solution(mesh):
    return jax.shard_map(
        on_device,
        mesh=mesh,
        in_specs=(P("dp", ("row", "col")), P("dp", ("row", "col"))),
        out_specs=(P(), P("dp", ("row", "col")), P("dp", ("row", "col"))),
        check_vma=False,
    )
```
